32 devices in a mesh: pipe: 4 (over z), ctx: 4 (over x, core), head: 2 (over y).
Axes of the slice: x: 2, y: 2, z: 4, core: 2. Of those that a mesh axis runs over, the one named last changes fastest.
Arguments:
- queries: bfloat16 [4, 512, 8192], P('pipe', 'ctx', 'head'), may hold values from -6 to 6
- key_states: bfloat16 [4, 512, 1024], P('pipe', 'ctx', 'head'), may hold values from -6 to 6
- value_states: bfloat16 [4, 512, 1024], P('pipe', 'ctx', 'head'), may hold values from -6 to 6
- upstream: bfloat16 [4, 512, 8192], P('pipe', ('ctx', 'head')), may hold values from -6 to 6
- selected: int32 [4, 8, 8, 8], P('pipe', 'head', 'ctx'), may hold values from 0 to 7, as said below
Outputs:
- query_grad: bfloat16 [4, 512, 8192], P('pipe', 'ctx', 'head')
- key_grad: bfloat16 [4, 512, 1024], P('pipe', 'ctx', 'head')
- value_grad: bfloat16 [4, 512, 1024], P('pipe', 'ctx', 'head')
The draws below stay inside these ranges and needn't reach their ends.
Inputs may be any that keep to these rules, and one draw needn't show every extreme that they name: `selected`: for query block b, entry 0 is b; the other 7 entries are distinct; min(b, 7) of them name blocks before b, the rest name blocks after b.
All inputs are finite; a program needn't handle non-finite values.
Results may differ from the reference program's by a relative error of at most 0.015.
Values may be sent and summed in bfloat16 or wider, within the bound.
No kernel may reach another device: no remote copies, remote signals or barrier semaphores. Data moves between devices by JAX's collectives and lax.ppermute only.
A program may use at most 64 MiB of HBM per device.

```python
import jax
import jax.numpy as jnp
from jax import lax

QH = 64
KVH = 8
HD = 128
BLK = 64
TOPB = 8
SECTIONS = 4
TOKENS = 512
QBLOCKS = 8
GROUP = 8


def draw_queries(key, part):
    own_key = jax.random.fold_in(key, 1)
    result = jnp.clip(jax.random.normal(own_key, (SECTIONS, TOKENS, QH * HD), jnp.float32), -6.0, 6.0)
    return result.astype(jnp.bfloat16)


def draw_key_states(key, part):
    own_key = jax.random.fold_in(key, 2)
    result = jnp.clip(jax.random.normal(own_key, (SECTIONS, TOKENS, KVH * HD), jnp.float32), -6.0, 6.0)
    return result.astype(jnp.bfloat16)


def draw_selected(key, part):
    own_key = jax.random.fold_in(key, 3)
    block_ids = jnp.arange(QBLOCKS, dtype=jnp.int32)
    earlier = block_ids[None, :] < block_ids[:, None]
    noise = jax.random.randint(own_key, (SECTIONS, KVH, QBLOCKS, QBLOCKS), 0, 1048576)
    ranking = jnp.where(earlier, noise * QBLOCKS + block_ids[None, :], block_ids[None, :] - 2 * QBLOCKS)
    picked = lax.top_k(ranking, TOPB - 1)[1].astype(jnp.int32)
    own_block = jnp.broadcast_to(block_ids[:, None], (SECTIONS, KVH, QBLOCKS, 1)).astype(jnp.int32)
    return jnp.concatenate([own_block, picked], axis=-1)


def shard_levels(key, dims, shards, smallest, high):
    gain, own = 1.0, jax.random.fold_in(key, 6)
    for axis_at, shards_of in shards:
        draws = jnp.exp(jax.random.uniform(jax.random.fold_in(own, axis_at), (shards_of,), jnp.float32, smallest / len(shards), high / len(shards)))
        gain = gain * jnp.repeat(draws, dims[axis_at] // shards_of).reshape([-1 if axis == axis_at else 1 for axis in range(len(dims))])
    return gain


def bell_draw(key, extent, width, bound, cuts=(), held_as=jnp.bfloat16):
    factor_of = shard_levels(key, extent, cuts, -0.22, 0.18) if cuts else 1.0
    values = jax.random.normal(key, extent, jnp.float32) * width * factor_of
    return jnp.minimum(jnp.maximum(values, -bound), bound).astype(held_as)


def setup_inputs(seed: int = 0) -> dict:
    arg_keys = jax.random.split(jax.random.key(seed), 6)
    queries = draw_queries(jax.random.fold_in(arg_keys[5], 71), 0)
    key_states = draw_key_states(jax.random.fold_in(arg_keys[5], 71), 0)
    value_states = bell_draw(arg_keys[2], (SECTIONS, TOKENS, KVH * HD), 1.0, 6.0, ((0, 4), (1, 4), (2, 2)))
    upstream = bell_draw(arg_keys[3], (SECTIONS, TOKENS, QH * HD), 1.0, 6.0, ((0, 4), (1, 8)))
    selected = draw_selected(jax.random.fold_in(arg_keys[5], 71), 0)
    return dict(queries=queries, key_states=key_states, value_states=value_states, upstream=upstream, selected=selected)


def section_grads(query_sec, key_sec, value_sec, grad_sec, chosen_sec):
    score_scale = HD ** -0.5
    query_tiles = query_sec.reshape(QBLOCKS, BLK, KVH, GROUP, HD)
    grad_tiles = grad_sec.reshape(QBLOCKS, BLK, KVH, GROUP, HD)
    key_table = key_sec.reshape(TOKENS, KVH, HD)
    value_table = value_sec.reshape(TOKENS, KVH, HD)
    offsets = jnp.arange(BLK, dtype=jnp.int32)
    head_index = jnp.arange(KVH, dtype=jnp.int32)[:, None]
    chosen = jnp.transpose(chosen_sec, (1, 0, 2))
    block_ids = jnp.arange(QBLOCKS, dtype=jnp.int32)

    def block_step(running, inputs):
        key_sums, value_sums = running
        query_blk, grad_blk, chosen_blk, block_index = inputs
        row_index = (chosen_blk[:, :, None] * BLK + offsets).reshape(KVH, TOPB * BLK)
        key_rows = key_table[row_index, head_index]
        value_rows = value_table[row_index, head_index]
        scores = jnp.einsum("icgh,cjh->cgij", query_blk.astype(jnp.float32), key_rows.astype(jnp.float32)) * score_scale
        query_pos = block_index * BLK + offsets
        visible = row_index[:, None, None, :] <= query_pos[None, None, :, None]
        scores = jnp.where(visible, scores, -jnp.inf)
        row_max = jnp.max(scores, axis=-1, keepdims=True)
        shifted = jnp.exp(scores - row_max)
        weights = shifted / jnp.sum(shifted, axis=-1, keepdims=True)
        weight_grad = jnp.einsum("icgh,cjh->cgij", grad_blk.astype(jnp.float32), value_rows.astype(jnp.float32))
        row_delta = jnp.sum(weights * weight_grad, axis=-1, keepdims=True)
        score_grad = (weights * (weight_grad - row_delta) * score_scale).astype(jnp.bfloat16)
        weight_half = weights.astype(jnp.bfloat16)
        query_part = jnp.einsum("cgij,cjh->icgh", score_grad.astype(jnp.float32), key_rows.astype(jnp.float32))
        key_part = jnp.einsum("cgij,icgh->cjh", score_grad.astype(jnp.float32), query_blk.astype(jnp.float32))
        value_part = jnp.einsum("cgij,icgh->cjh", weight_half.astype(jnp.float32), grad_blk.astype(jnp.float32))
        key_sums = key_sums.at[row_index, head_index].add(key_part)
        value_sums = value_sums.at[row_index, head_index].add(value_part)
        return (key_sums, value_sums), query_part.astype(jnp.bfloat16)

    start = (jnp.zeros((TOKENS, KVH, HD), jnp.float32), jnp.zeros((TOKENS, KVH, HD), jnp.float32))
    (key_sums, value_sums), query_parts = lax.scan(block_step, start, (query_tiles, grad_tiles, chosen, block_ids))
    query_grad = query_parts.reshape(TOKENS, QH * HD)
    key_grad = key_sums.reshape(TOKENS, KVH * HD).astype(jnp.bfloat16)
    value_grad = value_sums.reshape(TOKENS, KVH * HD).astype(jnp.bfloat16)
    return query_grad, key_grad, value_grad


def reference(queries, key_states, value_states, upstream, selected):
    out_grad = jnp.roll(upstream, -1, axis=0)

    def per_section(inputs):
        return section_grads(inputs[0], inputs[1], inputs[2], inputs[3], inputs[4])

    query_grad, key_grad, value_grad = lax.map(per_section, (queries, key_states, value_states, out_grad, selected))
    return query_grad, key_grad, value_grad
```

```python
import functools

import jax
import jax.numpy as jnp
from jax import lax
from jax.experimental import pallas as pl
from jax.experimental.pallas import tpu as pltpu
from jax.sharding import PartitionSpec as P

HD = 128
BLK = 64
GROUP = 8
PAIR = 2 * HD
HEAD_COLS = GROUP * HD
LOG2E = 1.4426950408889634
SCALE = HD**-0.5
VMEM = pltpu.MemorySpace.VMEM


def in_vmem():
    return pl.BlockSpec(memory_space=VMEM)


def contract(a, b, dims):
    return lax.dot_general(a, b, (dims, ((), ())), preferred_element_type=jnp.float32)


def two_heads(ref, column):
    wide = ref[:, pl.ds(pl.multiple_of(column, PAIR), PAIR)]
    return jnp.concatenate([wide[:, :HD], wide[:, HD:]], axis=0)


def stacked(refs, head):
    return jnp.concatenate([ref[:, head * HD : (head + 1) * HD] for ref in refs], axis=0)


def weights_kernel(slots, heads, q_ref, bias_ref, *refs):
    key_refs, out_ref = refs[:slots], refs[slots]
    tok_dev = q_ref.shape[0]
    keys = slots * tok_dev
    for head in range(heads):
        key_rows = stacked(key_refs, head)
        bias = bias_ref[head]
        bias = jnp.concatenate([bias, bias], axis=1)
        key_at = lax.broadcasted_iota(jnp.int32, (tok_dev, PAIR), 0)
        query_at = lax.broadcasted_iota(jnp.int32, (tok_dev, PAIR), 1) % tok_dev
        causal = key_at <= query_at

        def pair_step(pair, carry):
            rows = two_heads(q_ref, head * HEAD_COLS + pair * PAIR)
            scores = contract(key_rows, rows, ((1,), (1,))) * (SCALE * LOG2E)
            parts = []
            for kb in range(keys // BLK):
                part = scores[kb * BLK : (kb + 1) * BLK] + bias[kb : kb + 1]
                if kb * BLK < tok_dev:
                    part = jnp.where(causal[kb * BLK : (kb + 1) * BLK], part, -jnp.inf)
                parts.append(part)
            scores = jnp.concatenate(parts, axis=0)
            shifted = jnp.exp2(scores - jnp.max(scores, axis=0, keepdims=True))
            weights = shifted * (1.0 / jnp.sum(shifted, axis=0, keepdims=True))
            out_ref[head, :, pl.ds(pl.multiple_of(pair * PAIR, PAIR), PAIR)] = weights.astype(jnp.bfloat16)
            return carry

        lax.fori_loop(0, GROUP // 2, pair_step, 0)


def grads_kernel(slots, pieces, first, count, p_ref, q_ref, *refs):
    key_refs, refs = refs[:slots], refs[slots:]
    value_refs, refs = refs[:slots], refs[slots:]
    piece_refs, refs = refs[:pieces], refs[pieces:]
    dq_ref, keep_ref, send_ref, grad_ref, sum_ref = refs
    here = lax.axis_index("head")
    rows = piece_refs[0].shape[0]
    for step, piece in enumerate(piece_refs):
        source = lax.rem(here + pieces - step, pieces)
        grad_ref[pl.ds(pl.multiple_of(source * rows, rows), rows), :] = piece[...]
    half = send_ref.shape[0]
    for local in range(count):
        head = first + local
        key_rows = stacked(key_refs, head)
        value_rows = stacked(value_refs, head)
        sum_ref[...] = jnp.zeros_like(sum_ref)

        def pair_step(pair, carry):
            grads = two_heads(grad_ref, local * HEAD_COLS + pair * PAIR)
            queries = two_heads(q_ref, head * HEAD_COLS + pair * PAIR)
            half_weights = p_ref[head, :, pl.ds(pl.multiple_of(pair * PAIR, PAIR), PAIR)]
            weights = half_weights.astype(jnp.float32)
            weight_grad = contract(value_rows, grads, ((1,), (1,)))
            delta = jnp.sum(weights * weight_grad, axis=0, keepdims=True)
            score_grad = (weights * (weight_grad - delta)).astype(jnp.bfloat16)
            sum_ref[:, :HD] += contract(score_grad, queries, ((1,), (0,)))
            sum_ref[:, HD:] += contract(half_weights, grads, ((1,), (0,)))
            turned = contract(key_rows, score_grad, ((0,), (0,))) * SCALE
            tokens = turned.shape[1] // 2
            query_grad = jnp.concatenate([turned[:, :tokens].T, turned[:, tokens:].T], axis=1)
            column = pl.multiple_of(local * HEAD_COLS + pair * PAIR, PAIR)
            dq_ref[:, pl.ds(column, PAIR)] = query_grad.astype(jnp.bfloat16)
            return carry

        lax.fori_loop(0, GROUP // 2, pair_step, 0)
        for at, factor in ((0, SCALE), (1, 1.0)):
            total = sum_ref[:, at * HD : (at + 1) * HD] * factor
            columns = slice((at * count + local) * HD, (at * count + local + 1) * HD)
            keep_ref[:, columns] = total[:half]
            send_ref[:, columns] = total[half:].astype(jnp.bfloat16)


def per_device(queries, key_states, value_states, upstream, selected):
    ctx, here = lax.axis_size("ctx"), lax.axis_index("ctx")
    pipe, split = lax.axis_size("pipe"), lax.axis_size("head")
    head_place = lax.axis_index("head")
    tok_dev = queries.shape[1]
    heads = key_states.shape[2] // HD
    blocks = tok_dev // BLK
    chunks = [(0, 2), (2, 1), (3, 1)] if heads == 4 else [(at, 1) for at in range(heads)]

    def swapped(value, mask):
        return lax.ppermute(value, "ctx", [(place, place ^ mask) for place in range(ctx)])

    def arriving(first, count):
        pieces = []
        for step in range(split):
            route = [
                (sec * split + at, (sec - 1) % pipe * split + (at + step) % split)
                for sec in range(pipe)
                for at in range(split)
            ]
            target = lax.rem(head_place + step, split)
            start = (target * heads + first) * HEAD_COLS
            part = lax.dynamic_slice_in_dim(upstream[0], start, count * HEAD_COLS, 1)
            pieces.append(lax.ppermute(part, ("pipe", "head"), route))
        return pieces

    pieces = [arriving(first, count) for first, count in chunks]

    masks = [1 << bit for bit in reversed(range(ctx.bit_length() - 1))]
    order = [0]
    key_slots, value_slots = [key_states[0]], [value_states[0]]
    for mask in masks:
        order = order + [slot ^ mask for slot in order]
        key_slots = key_slots + [swapped(part, mask) for part in key_slots]
        value_slots = value_slots + [swapped(part, mask) for part in value_slots]

    slot_owner = here ^ jnp.array(order, dtype=jnp.int32)
    key_block = (slot_owner[:, None] * blocks + jnp.arange(blocks, dtype=jnp.int32)).reshape(-1)
    query_block = here * blocks + jnp.arange(blocks, dtype=jnp.int32)
    chosen = jnp.any(selected[0][:, :, :, None] == key_block, axis=2)
    usable = chosen & (key_block[None, None, :] <= query_block[None, :, None])
    bias = jnp.where(usable, 0.0, -jnp.inf).astype(jnp.float32)
    bias = jnp.repeat(jnp.transpose(bias, (0, 2, 1)), BLK, axis=2)

    slots = len(order)
    keys = slots * tok_dev
    rows = GROUP * tok_dev
    weights = pl.pallas_call(
        functools.partial(weights_kernel, slots, heads),
        out_shape=jax.ShapeDtypeStruct((heads, keys, rows), jnp.bfloat16),
        in_specs=[in_vmem()] * (2 + slots),
        out_specs=in_vmem(),
        name="weights",
        cost_estimate=pl.CostEstimate(
            flops=2 * heads * keys * rows * HD, bytes_accessed=8 << 20, transcendentals=heads * keys * rows
        ),
        compiler_params=pltpu.CompilerParams(vmem_limit_bytes=24 << 20),
    )(queries[0], bias, *key_slots)

    query_parts, key_parts, value_parts = [], [], []
    for (first, count), parts in zip(chunks, pieces):
        width = 2 * count * HD
        query_part, keep, send = pl.pallas_call(
            functools.partial(grads_kernel, slots, split, first, count),
            out_shape=(
                jax.ShapeDtypeStruct((tok_dev, count * HEAD_COLS), jnp.bfloat16),
                jax.ShapeDtypeStruct((keys // 2, width), jnp.float32),
                jax.ShapeDtypeStruct((keys // 2, width), jnp.bfloat16),
            ),
            in_specs=[in_vmem()] * (2 + 2 * slots + split),
            out_specs=(in_vmem(),) * 3,
            scratch_shapes=[
                pltpu.VMEM((tok_dev, count * HEAD_COLS), jnp.bfloat16),
                pltpu.VMEM((keys, 2 * HD), jnp.float32),
            ],
            name=f"grads_{first}",
            cost_estimate=pl.CostEstimate(
                flops=8 * count * keys * rows * HD, bytes_accessed=4 << 20, transcendentals=0
            ),
            compiler_params=pltpu.CompilerParams(vmem_limit_bytes=24 << 20),
        )(weights, queries[0], *key_slots, *value_slots, *parts)
        query_parts.append(query_part)
        for mask in reversed(masks):
            total = keep + swapped(send, mask).astype(jnp.float32)
            half = total.shape[0] // 2
            if mask != masks[0]:
                keep, send = total[:half], total[half:].astype(jnp.bfloat16)
            else:
                keep = total
        key_parts.append(keep[:, : width // 2].astype(jnp.bfloat16))
        value_parts.append(keep[:, width // 2 :].astype(jnp.bfloat16))
    query_grad = jnp.concatenate(query_parts, axis=1)[None]
    key_grad = jnp.concatenate(key_parts, axis=1)[None]
    value_grad = jnp.concatenate(value_parts, axis=1)[None]
    return query_grad, key_grad, value_grad


def solution(mesh):
    split = P("pipe", "ctx", "head")
    placed = (split, split, split, P("pipe", ("ctx", "head"), None), P("pipe", "head", "ctx", None))
    return jax.shard_map(
        per_device, mesh=mesh, in_specs=placed, out_specs=(split, split, split), check_vma=False
    )
```

```python
import functools

import jax
import jax.numpy as jnp
from jax import lax
from jax.experimental import pallas as pl
from jax.experimental.pallas import tpu as pltpu
from jax.sharding import PartitionSpec as P

HD = 128
BLK = 64
GROUP = 8
HEAD_COLS = GROUP * HD
LOG2E = 1.4426950408889634
SCALE = HD**-0.5
VMEM = pltpu.MemorySpace.VMEM
HBM = pltpu.MemorySpace.HBM
BF16 = jnp.bfloat16
F32 = jnp.float32


def spec(space=VMEM):
    return pl.BlockSpec(memory_space=space)


def in_hbm(value):
    return pltpu.with_memory_space_constraint(value, HBM)


def shape(dims, dtype=BF16):
    return jax.ShapeDtypeStruct(dims, dtype)


def call(body, name, out_shape, in_specs, out_specs, traffic=1024, **rest):
    return pl.pallas_call(
        body,
        out_shape=out_shape,
        in_specs=in_specs,
        out_specs=out_specs,
        name=name,
        cost_estimate=pl.CostEstimate(flops=1024, bytes_accessed=traffic, transcendentals=0),
        compiler_params=pltpu.CompilerParams(vmem_limit_bytes=24 << 20),
        **rest,
    )


def contract(a, b, dims):
    return lax.dot_general(a, b, (dims, ((), ())), preferred_element_type=F32)


def head_rows(ref, head):
    first = head * HEAD_COLS
    return jnp.concatenate([ref[:, first + g * HD : first + (g + 1) * HD] for g in range(GROUP)], axis=0)


def key_rows(refs, head):
    return jnp.concatenate([ref[:, head * HD : (head + 1) * HD] for ref in refs], axis=0)


def value_rows(refs, head):
    first = refs[0].shape[1] // 2 + head * HD
    return jnp.concatenate([ref[:, first : first + HD] for ref in refs], axis=0)


def store_rows(ref, column, turned):
    rows = ref.shape[0]
    for g in range(GROUP):
        ref[:, column + g * HD : column + (g + 1) * HD] = turned[:, g * rows : (g + 1) * rows].T


def run_copies(copies, sem):
    copies = [pltpu.make_async_copy(src, dst, sem.at[at]) for at, (src, dst) in enumerate(copies)]
    for copy in copies:
        copy.start()
    for copy in copies:
        copy.wait()


def cut_copies(sends, split, heads, up_ref, piece_refs):
    here = lax.axis_index("head")
    copies = []
    for at, (first, count) in enumerate(sends):
        for step in range(split):
            target = lax.rem(here + step, split)
            start = pl.multiple_of((target * heads * GROUP + first) * HD, HD)
            copies.append((up_ref.at[:, pl.ds(start, count * HD)], piece_refs[at * split + step]))
    return copies


def first_load_kernel(sends, split, heads, up_ref, k_ref, v_ref, *refs):
    *piece_refs, kv_out, sem = refs
    wide = k_ref.shape[1]
    copies = [(k_ref, kv_out.at[:, :wide]), (v_ref, kv_out.at[:, wide:])]
    run_copies(copies + cut_copies(sends, split, heads, up_ref, piece_refs), sem)


def later_load_kernel(sends, split, heads, up_ref, q_ref, *refs):
    *piece_refs, q_out, sem = refs
    run_copies([*cut_copies(sends, split, heads, up_ref, piece_refs), (q_ref, q_out)], sem)


def block_bias(order, selected_ref, head, tok_dev):
    blocks = tok_dev // BLK
    total = len(order) * blocks
    here = lax.axis_index("ctx")
    at = lax.broadcasted_iota(jnp.int32, (total, 1), 0)
    slot = jnp.zeros_like(at)
    for index, mask in enumerate(order):
        slot = jnp.where(at // blocks == index, mask, slot)
    key_block = (here ^ slot) * blocks + at % blocks
    columns = []
    for qb in range(blocks):
        hit = jnp.where(selected_ref[head, qb : qb + 1, :] == key_block, 1, 0)
        chosen = jnp.max(hit, axis=1, keepdims=True) > 0
        bias = jnp.where(chosen & (key_block <= here * blocks + qb), 0.0, -jnp.inf)
        columns.append(jnp.broadcast_to(bias, (total, BLK)))
    return jnp.concatenate(columns * GROUP, axis=1)


def weights_kernel(order, heads, q_ref, selected_ref, *refs):
    kv_refs, p_ref = refs[:-1], refs[-1]
    tok_dev = q_ref.shape[0]
    rows = GROUP * tok_dev
    keys = len(order) * tok_dev
    key_at = lax.broadcasted_iota(jnp.int32, (tok_dev, rows), 0)
    query_at = lax.broadcasted_iota(jnp.int32, (tok_dev, rows), 1) % tok_dev
    causal = key_at <= query_at
    for head in range(heads):
        bias = block_bias(order, selected_ref, head, tok_dev)
        scores = contract(key_rows(kv_refs, head), head_rows(q_ref, head), ((1,), (1,)))
        scores = scores * (SCALE * LOG2E)
        parts = []
        for kb in range(keys // BLK):
            part = scores[kb * BLK : (kb + 1) * BLK] + bias[kb : kb + 1]
            if kb * BLK < tok_dev:
                part = jnp.where(causal[kb * BLK : (kb + 1) * BLK], part, -jnp.inf)
            parts.append(part)
        scores = jnp.concatenate(parts, axis=0)
        shifted = jnp.exp2(scores - jnp.max(scores, axis=0, keepdims=True))
        p_ref[head] = (shifted * (1.0 / jnp.sum(shifted, axis=0, keepdims=True))).astype(BF16)


def outs_kernel(heads, p_ref, *refs):
    kv_refs, o_ref = refs[:-1], refs[-1]
    for head in range(heads):
        turned = contract(value_rows(kv_refs, head).T, p_ref[head], ((1,), (0,))).astype(BF16)
        store_rows(o_ref, head * HEAD_COLS, turned)


def overlaps(sends, first, count):
    begin, end = first * GROUP, (first + count) * GROUP
    return [at for at, (start, size) in enumerate(sends) if start < end and start + size > begin]


def put_pieces(sends, first, split, grad_ref, piece_refs):
    here = lax.axis_index("head")
    begin, width = first * GROUP, grad_ref.shape[1] // HD
    for at, index in enumerate(overlaps(sends, first, width // GROUP)):
        start, size = sends[index]
        low, high = max(start, begin), min(start + size, begin + width)
        for step in range(split):
            piece = piece_refs[at * split + step]
            rows = piece.shape[0]
            source = lax.rem(here + split - step, split)
            grad_ref[
                pl.ds(pl.multiple_of(source * rows, rows), rows), (low - begin) * HD : (high - begin) * HD
            ] = piece[:, (low - start) * HD : (high - start) * HD]


def head_grads(head, grads, p_ref, o_ref, q_ref, value_rows, first, last):
    queries, outs = head_rows(q_ref, head), head_rows(o_ref, head)
    delta = (grads.astype(F32) * outs.astype(F32)).astype(BF16)
    weights = p_ref[head, first:last]
    left = jnp.concatenate([value_rows, jnp.full(value_rows.shape, -1, BF16)], axis=1)
    centred = contract(left, jnp.concatenate([grads, delta], axis=1), ((1,), (1,)))
    score_grad = (weights.astype(F32) * centred).astype(BF16)
    key_part = contract(score_grad, queries, ((1,), (0,))) * SCALE
    value_part = contract(weights, grads, ((1,), (0,)))
    return score_grad, key_part, value_part


def put_query_grad(head, keys_of_head, score_grad, stage_ref, column, dq_ref, sem):
    turned = (contract(keys_of_head.T, score_grad, ((1,), (0,))) * SCALE).astype(BF16)
    store_rows(stage_ref, column, turned)
    copy = pltpu.make_async_copy(
        stage_ref.at[:, column : column + HEAD_COLS],
        dq_ref.at[:, head * HEAD_COLS : (head + 1) * HEAD_COLS],
        sem,
    )
    copy.start()
    return copy


def put_sums(ref, count, local, key_part, value_part):
    ref[:, local * HD : (local + 1) * HD] = key_part.astype(ref.dtype)
    ref[:, (count + local) * HD : (count + local + 1) * HD] = value_part.astype(ref.dtype)


def chunk_kernel(order, sends, split, first, count, aliased, p_ref, o_ref, q_ref, *refs):
    slots = len(order)
    kv_refs, refs = refs[:slots], refs[slots:]
    piece_refs, (dq_ref, keep_ref, send_ref, grad_ref, stage_ref, sem) = refs[: -6 - aliased], refs[-6:]
    put_pieces(sends, first, split, grad_ref, piece_refs)
    half = keep_ref.shape[0]
    copies = []
    for local in range(count):
        head = first + local
        score_grad, key_part, value_part = head_grads(
            head, head_rows(grad_ref, local), p_ref, o_ref, q_ref, value_rows(kv_refs, head), 0, 2 * half
        )
        keys_of_head = key_rows(kv_refs, head)
        copies.append(
            put_query_grad(
                head, keys_of_head, score_grad, stage_ref, local * HEAD_COLS, dq_ref, sem.at[local]
            )
        )
        tok_dev = q_ref.shape[0]
        for ref, slots_of in ((keep_ref, range(slots // 2)), (send_ref, range(slots // 2, slots))):
            for at, slot in enumerate(slots_of):
                part = slice(order.index(slot) * tok_dev, (order.index(slot) + 1) * tok_dev)
                put_sums(
                    ref.at[at * tok_dev : (at + 1) * tok_dev], count, local, key_part[part], value_part[part]
                )
    for copy in copies:
        copy.wait()


def half_kernel(half, sends, split, first, count, begin, p_ref, o_ref, q_ref, *refs):
    kv_refs, refs = refs[:half], refs[half:]
    if split:
        piece_refs, (ds_ref, sums_ref, grad_ref) = refs[:-3], refs[-3:]
        put_pieces(sends, first, split, grad_ref, piece_refs)
    else:
        grad_ref, ds_ref, sums_ref = refs
    for local in range(count):
        head = first + local
        score_grad, key_part, value_part = head_grads(
            head,
            head_rows(grad_ref, local),
            p_ref,
            o_ref,
            q_ref,
            value_rows(kv_refs, head),
            begin,
            begin + sums_ref.shape[0],
        )
        ds_ref[local] = score_grad
        put_sums(sums_ref, count, local, key_part, value_part)


def query_kernel(slots, first, count, aliased, near_ref, far_ref, *refs):
    kv_refs, (dq_ref, stage_ref, sem) = refs[:slots], refs[slots + aliased :]
    copies = []
    for local in range(count):
        score_grad = jnp.concatenate([near_ref[local], far_ref[local]], axis=0)
        keys_of_head = key_rows(kv_refs, first + local)
        copies.append(
            put_query_grad(
                first + local, keys_of_head, score_grad, stage_ref, local * HEAD_COLS, dq_ref, sem.at[local]
            )
        )
    for copy in copies:
        copy.wait()


def add_kernel(keep_ref, received_ref, *refs):
    total = keep_ref[...] + received_ref[...].astype(F32)
    half = refs[0].shape[0]
    refs[0][...] = total[:half]
    refs[1][...] = total[half:].astype(BF16)


def finish_kernel(groups, *refs):
    key_ref, value_ref = refs[-2:]
    for at, (first, count) in enumerate(groups):
        total = refs[2 * at][...] + refs[2 * at + 1][...].astype(F32)
        key_ref[:, first * HD : (first + count) * HD] = total[:, : count * HD].astype(BF16)
        value_ref[:, first * HD : (first + count) * HD] = total[:, count * HD :].astype(BF16)


def per_device(queries, key_states, value_states, upstream, selected):
    ctx = lax.axis_size("ctx")
    pipe, split = lax.axis_size("pipe"), lax.axis_size("head")
    tok_dev, rows_in = queries.shape[1], upstream.shape[1]
    heads = key_states.shape[2] // HD
    groups = [(0, 2), (2, 2)] if heads == 4 else [(head, 1) for head in range(heads)]
    sends = [(0, 18), (18, 14)] if heads == 4 else [(head * GROUP, GROUP) for head in range(heads)]

    def swapped(value, mask):
        return lax.ppermute(value, "ctx", [(place, place ^ mask) for place in range(ctx)])

    def across(parts):
        for step in range(split):
            route = [
                (sec * split + at, (sec - 1) % pipe * split + (at + step) % split)
                for sec in range(pipe)
                for at in range(split)
            ]
            yield lax.ppermute(parts[step], ("pipe", "head"), route)

    wide = heads * HD
    up, own_queries, own_keys, own_values = (
        in_hbm(value[0]) for value in (upstream, queries, key_states, value_states)
    )

    def cut_shapes(sends):
        return [shape((rows_in, count * HD)) for _, count in sends for _ in range(split)]

    *cut, own_kv = call(
        functools.partial(first_load_kernel, sends[:1], split, heads),
        "first_load",
        [*cut_shapes(sends[:1]), shape((tok_dev, 2 * wide))],
        [spec(HBM)] * 3,
        [spec()] * (split + 1),
        scratch_shapes=[pltpu.SemaphoreType.DMA((split + 2,))],
    )(up, own_keys, own_values)
    later = (len(sends) - 1) * split
    *more, own_queries = call(
        functools.partial(later_load_kernel, sends[1:], split, heads),
        "later_load",
        [*cut_shapes(sends[1:]), shape(queries.shape[1:])],
        [spec(HBM)] * 2,
        [spec()] * (later + 1),
        scratch_shapes=[pltpu.SemaphoreType.DMA((later + 1,))],
    )(up, own_queries)
    cut = cut + more
    pieces = [list(across(cut[at * split : (at + 1) * split])) for at in range(len(sends))]

    def pieces_of(first, count):
        return [piece for at in overlaps(sends, first, count) for piece in pieces[at]]

    masks = [1 << bit for bit in reversed(range(ctx.bit_length() - 1))]
    order = [0]
    for mask in masks:
        order = order + [slot ^ mask for slot in order]

    kv = [own_kv, *(swapped(own_kv, slot) for slot in order[1:])]

    slots = ctx
    keys, rows = slots * tok_dev, GROUP * tok_dev
    half = keys // 2
    weights = call(
        functools.partial(weights_kernel, order, heads),
        "weights",
        shape((heads, keys, rows)),
        [spec()] * (2 + slots),
        spec(),
    )(own_queries, selected[0], *kv)
    outs = call(
        functools.partial(outs_kernel, heads),
        "outs",
        shape((tok_dev, heads * HEAD_COLS)),
        [spec()] * (1 + slots),
        spec(),
    )(weights, *kv)

    given = (weights, outs, own_queries)
    query_shape = shape((tok_dev, heads * HEAD_COLS))
    query_grad = None

    def combined(keep, send, masks):
        for mask in masks:
            received = swapped(send, mask)
            if mask == masks[-1]:
                return keep, received
            part = (keep.shape[0] // 2, keep.shape[1])
            keep, send = call(
                add_kernel, "add", [shape(part, F32), shape(part)], [spec()] * 2, [spec()] * 2
            )(keep, received)

    sums, early = [], []
    for first, count in groups[:-1]:
        before = () if query_grad is None else (query_grad,)
        ins = (*given, *kv, *pieces_of(first, count))
        query_grad, keep, send = call(
            functools.partial(chunk_kernel, order, sends, split, first, count, len(before)),
            f"grads_{first}",
            [query_shape, shape((half, 2 * count * HD), F32), shape((half, 2 * count * HD))],
            [spec()] * len(ins) + [spec(HBM)] * len(before),
            [spec(HBM), spec(), spec()],
            scratch_shapes=[
                pltpu.VMEM((tok_dev, count * HEAD_COLS), BF16),
                pltpu.VMEM((tok_dev, count * HEAD_COLS), BF16),
                pltpu.SemaphoreType.DMA((count,)),
            ],
            input_output_aliases={len(ins): 0} if before else {},
        )(*ins, *before)
        early.append(send)
        sums.extend(combined(keep, send, masks))

    first, count = groups[-1]
    sum_cols = 2 * count * HD
    ins = (*given, *kv[slots // 2 :], *pieces_of(first, count), *early)
    far_scores, send, grads = call(
        functools.partial(half_kernel, slots // 2, sends, split, first, count, half),
        "sums_sent",
        [shape((count, half, rows)), shape((half, sum_cols)), shape((tok_dev, count * HEAD_COLS))],
        [spec()] * len(ins),
        [spec()] * 3,
    )(*ins)
    ins = (*given, *kv[: slots // 2], grads)
    near_scores, keep = call(
        functools.partial(half_kernel, slots // 2, sends, 0, first, count, 0),
        "sums_kept",
        [shape((count, half, rows)), shape((half, sum_cols), F32)],
        [spec()] * len(ins),
        [spec()] * 2,
        traffic=3 << 20,
    )(*ins)
    before = () if query_grad is None else (query_grad,)
    ins = (near_scores, far_scores, *kv)
    query_grad = call(
        functools.partial(query_kernel, slots, first, count, len(before)),
        "query",
        query_shape,
        [spec()] * len(ins) + [spec(HBM)] * len(before),
        spec(HBM),
        traffic=4 << 20,
        scratch_shapes=[pltpu.VMEM((tok_dev, count * HEAD_COLS), BF16), pltpu.SemaphoreType.DMA((count,))],
        input_output_aliases={len(ins): 0} if before else {},
    )(*ins, *before)
    sums.extend(combined(keep, send, masks[::-1]))

    key_grad, value_grad = call(
        functools.partial(finish_kernel, groups),
        "finish",
        [shape((tok_dev, wide))] * 2,
        [spec()] * len(sums),
        [spec()] * 2,
    )(*sums)
    return query_grad[None], key_grad[None], value_grad[None]


def solution(mesh):
    split = P("pipe", "ctx", "head")
    placed = (split, split, split, P("pipe", ("ctx", "head"), None), P("pipe", "head", "ctx", None))
    return jax.shard_map(
        per_device, mesh=mesh, in_specs=placed, out_specs=(split, split, split), check_vma=False
    )
```

```python
import functools

import jax
import jax.numpy as jnp
from jax import lax
from jax.experimental import pallas as pl
from jax.experimental.pallas import tpu as pltpu
from jax.sharding import PartitionSpec as P

HD = 128
BLK = 64
GROUP = 8
HEAD_COLS = GROUP * HD
LOG2E = 1.4426950408889634
SCALE = HD**-0.5
VMEM = pltpu.MemorySpace.VMEM
HBM = pltpu.MemorySpace.HBM
BF16 = jnp.bfloat16
F32 = jnp.float32


def spec(space=VMEM):
    return pl.BlockSpec(memory_space=space)


def in_hbm(value):
    return pltpu.with_memory_space_constraint(value, HBM)


def shape(dims, dtype=BF16):
    return jax.ShapeDtypeStruct(dims, dtype)


def call(body, name, out_shape, in_specs, out_specs, **rest):
    return pl.pallas_call(
        body,
        out_shape=out_shape,
        in_specs=in_specs,
        out_specs=out_specs,
        name=name,
        cost_estimate=pl.CostEstimate(flops=1024, bytes_accessed=1024, transcendentals=0),
        compiler_params=pltpu.CompilerParams(vmem_limit_bytes=24 << 20),
        **rest,
    )


def contract(a, b, dims):
    return lax.dot_general(a, b, (dims, ((), ())), preferred_element_type=F32)


def head_rows(ref, head):
    first = head * HEAD_COLS
    return jnp.concatenate([ref[:, first + g * HD : first + (g + 1) * HD] for g in range(GROUP)], axis=0)


def key_rows(kv_refs, head):
    return jnp.concatenate([ref[:, head * HD : (head + 1) * HD] for ref in kv_refs], axis=0)


def value_rows(kv_refs, head):
    first = kv_refs[0].shape[1] // 2 + head * HD
    return jnp.concatenate([ref[:, first : first + HD] for ref in kv_refs], axis=0)


def store_rows(ref, column, turned):
    rows = ref.shape[0]
    for g in range(GROUP):
        ref[:, column + g * HD : column + (g + 1) * HD] = turned[:, g * rows : (g + 1) * rows].T


def run_copies(copies, sem):
    copies = [pltpu.make_async_copy(src, dst, sem.at[at]) for at, (src, dst) in enumerate(copies)]
    for copy in copies:
        copy.start()
    for copy in copies:
        copy.wait()


def cut_copies(sends, split, heads, up_ref, piece_refs):
    here = lax.axis_index("head")
    copies = []
    for at, (first, count) in enumerate(sends):
        for step in range(split):
            target = lax.rem(here + step, split)
            start = pl.multiple_of((target * heads * GROUP + first) * HD, HD)
            copies.append((up_ref.at[:, pl.ds(start, count * HD)], piece_refs[at * split + step]))
    return copies


def first_load_kernel(sends, split, heads, up_ref, k_ref, v_ref, *refs):
    *piece_refs, kv_out, sem = refs
    wide = k_ref.shape[1]
    copies = cut_copies(sends, split, heads, up_ref, piece_refs)
    run_copies([*copies, (k_ref, kv_out.at[:, :wide]), (v_ref, kv_out.at[:, wide:])], sem)


def later_load_kernel(sends, split, heads, others, up_ref, q_ref, *refs):
    other_refs, (*piece_refs, q_out), other_outs, sem = (
        refs[:others],
        refs[others : -1 - others],
        refs[-1 - others : -1],
        refs[-1],
    )
    copies = cut_copies(sends, split, heads, up_ref, piece_refs)
    run_copies([*copies, *zip(other_refs, other_outs), (q_ref, q_out)], sem)


def overlaps(sends, first, count):
    begin, end = first * GROUP, (first + count) * GROUP
    return [at for at, (start, size) in enumerate(sends) if start < end and start + size > begin]


def put_pieces(sends, first, split, grad_ref, piece_refs):
    here = lax.axis_index("head")
    begin, width = first * GROUP, grad_ref.shape[1] // HD
    for at, index in enumerate(overlaps(sends, first, width // GROUP)):
        start, size = sends[index]
        low, high = max(start, begin), min(start + size, begin + width)
        for step in range(split):
            piece = piece_refs[at * split + step]
            rows = piece.shape[0]
            source = lax.rem(here + split - step, split)
            grad_ref[
                pl.ds(pl.multiple_of(source * rows, rows), rows), (low - begin) * HD : (high - begin) * HD
            ] = piece[:, (low - start) * HD : (high - start) * HD]


def block_bias(slots, selected_ref, head, tok_dev):
    blocks = tok_dev // BLK
    here = lax.axis_index("ctx")
    at = lax.broadcasted_iota(jnp.int32, (slots * blocks, 1), 0)
    key_block = (here ^ (at // blocks)) * blocks + at % blocks
    columns = []
    for qb in range(blocks):
        hit = jnp.where(selected_ref[head, qb : qb + 1, :] == key_block, 1, 0)
        chosen = jnp.max(hit, axis=1, keepdims=True) > 0
        bias = jnp.where(chosen & (key_block <= here * blocks + qb), 0.0, -jnp.inf)
        columns.append(jnp.broadcast_to(bias, (slots * blocks, BLK)))
    return jnp.concatenate(columns * GROUP, axis=1)


def weights_kernel(slots, heads, q_ref, selected_ref, *refs):
    kv_refs, (p_ref, o_ref) = refs[:slots], refs[slots:]
    tok_dev = q_ref.shape[0]
    rows = GROUP * tok_dev
    key_at = lax.broadcasted_iota(jnp.int32, (tok_dev, rows), 0)
    query_at = lax.broadcasted_iota(jnp.int32, (tok_dev, rows), 1) % tok_dev
    causal = key_at <= query_at
    for head in range(heads):
        bias = block_bias(slots, selected_ref, head, tok_dev)
        scores = contract(key_rows(kv_refs, head), head_rows(q_ref, head), ((1,), (1,)))
        scores = scores * (SCALE * LOG2E)
        parts = []
        for kb in range(slots * tok_dev // BLK):
            part = scores[kb * BLK : (kb + 1) * BLK] + bias[kb : kb + 1]
            if kb * BLK < tok_dev:
                part = jnp.where(causal[kb * BLK : (kb + 1) * BLK], part, -jnp.inf)
            parts.append(part)
        scores = jnp.concatenate(parts, axis=0)
        shifted = jnp.exp2(scores - jnp.max(scores, axis=0, keepdims=True))
        weights = (shifted * (1.0 / jnp.sum(shifted, axis=0, keepdims=True))).astype(BF16)
        p_ref[head] = weights
        turned = contract(value_rows(kv_refs, head).T, weights, ((1,), (0,))).astype(BF16)
        store_rows(o_ref, head * HEAD_COLS, turned)


def sums_kernel(slots, first, count, sends, split, before, layout, p_ref, o_ref, q_ref, *refs):
    begin, end = slots
    kv_refs, refs = refs[: end - begin], refs[end - begin :]
    if before:
        for ref, done_ref, (_, _, kinds) in zip(refs[-len(layout) :], refs, layout):
            for at in range(len(kinds)):
                to = at * (before + count) * HD
                ref[:, to : to + before * HD] = done_ref[:, at * before * HD : (at + 1) * before * HD]
        refs = refs[len(layout) :]
    if split:
        piece_refs = refs[: -2 - len(layout)]
        grad_ref, ds_ref, *sum_refs = refs[-2 - len(layout) :]
        put_pieces(sends, first, split, grad_ref, piece_refs)
    else:
        grad_ref, ds_ref, *sum_refs = refs[0], *refs[-1 - len(layout) :]
    tok_dev = q_ref.shape[0]
    for local in range(count):
        head = first + local
        grads, queries, outs = head_rows(grad_ref, local), head_rows(q_ref, head), head_rows(o_ref, head)
        delta = (grads.astype(F32) * outs.astype(F32)).astype(BF16)
        weights = p_ref[head, begin * tok_dev : end * tok_dev]
        values = value_rows(kv_refs, head)
        left = jnp.concatenate([values, jnp.full(values.shape, -1, BF16)], axis=1)
        centred = contract(left, jnp.concatenate([grads, delta], axis=1), ((1,), (1,)))
        score_grad = (weights.astype(F32) * centred).astype(BF16)
        ds_ref[local] = score_grad
        sums = {
            "key": contract(score_grad, queries, ((1,), (0,))) * SCALE,
            "value": contract(weights, grads, ((1,), (0,))),
        }
        for ref, (from_slot, to_slot, kinds) in zip(sum_refs, layout):
            for at, kind in enumerate(kinds):
                column = (at * (before + count) + before + local) * HD
                part = sums[kind][(from_slot - begin) * tok_dev : (to_slot - begin) * tok_dev]
                ref[:, column : column + HD] = part.astype(ref.dtype)


def query_kernel(slots, places, parts, *refs):
    ds_refs, kv_refs, (dq_ref, stage_ref, sem) = refs[:parts], refs[parts : parts + slots], refs[-3:]
    copies = []
    for head, (found, row) in enumerate(places):
        score_grad = jnp.concatenate([ds_refs[at][row] for at in found], axis=0)
        turned = (contract(key_rows(kv_refs, head).T, score_grad, ((1,), (0,))) * SCALE).astype(BF16)
        store_rows(stage_ref, head * HEAD_COLS, turned)
        columns = slice(head * HEAD_COLS, (head + 1) * HEAD_COLS)
        copies.append(
            pltpu.make_async_copy(stage_ref.at[:, columns], dq_ref.at[:, columns], sem.at[head])
        )
        copies[-1].start()
    for copy in copies:
        copy.wait()


def add_kernel(outs, keep_ref, received_ref, *refs):
    total = keep_ref[...] + received_ref[...].astype(F32)
    done = 0
    for ref in refs[-outs:]:
        ref[...] = total[done : done + ref.shape[0]].astype(ref.dtype)
        done += ref.shape[0]


def finish_kernel(groups, counts, *refs):
    key_ref, value_ref = refs[-2:]
    refs = list(refs[:-2])
    for (first, count), (whole, halves) in zip(groups, counts):
        parts, refs = refs[: whole + 2 * halves], refs[whole + 2 * halves :]
        width = count * HD
        keys = [ref[:, :width] for ref in parts[:whole]] + [ref[...] for ref in parts[whole::2]]
        values = [ref[:, width:] for ref in parts[:whole]] + [ref[...] for ref in parts[whole + 1 :: 2]]
        for ref, found in ((key_ref, keys), (value_ref, values)):
            total = sum(part.astype(F32) for part in found[1:]) + found[0]
            ref[:, first * HD : (first + count) * HD] = total.astype(BF16)


def per_device(queries, key_states, value_states, upstream, selected):
    slots = lax.axis_size("ctx")
    pipe, split = lax.axis_size("pipe"), lax.axis_size("head")
    tok_dev, rows_in = queries.shape[1], upstream.shape[1]
    heads = key_states.shape[2] // HD
    wide, rows = heads * HD, GROUP * tok_dev
    paired = heads == 4 and slots == 4
    groups = [(0, 2), (2, 2)] if paired else [(0, heads)]
    sends = [(0, 24), (24, 8)] if paired else [(0, heads * GROUP)]

    def swapped(value, mask):
        return lax.ppermute(value, "ctx", [(place, place ^ mask) for place in range(slots)])

    def across(part, step):
        route = [
            (sec * split + at, (sec - 1) % pipe * split + (at + step) % split)
            for sec in range(pipe)
            for at in range(split)
        ]
        return lax.ppermute(part, ("pipe", "head"), route)

    up, own_queries, own_keys, own_values = (
        in_hbm(value[0]) for value in (upstream, queries, key_states, value_states)
    )

    def cut_shapes(sends):
        return [shape((rows_in, count * HD)) for _, count in sends for _ in range(split)]

    *cut, own_kv = call(
        functools.partial(first_load_kernel, sends[:1], split, heads),
        "first_load",
        [*cut_shapes(sends[:1]), shape((tok_dev, 2 * wide))],
        [spec(HBM)] * 3,
        [spec()] * (split + 1),
        scratch_shapes=[pltpu.SemaphoreType.DMA((split + 2,))],
    )(up, own_keys, own_values)

    def gathered(own):
        found = {0: own}
        for mask in [1 << bit for bit in reversed(range(slots.bit_length() - 1))]:
            found.update({slot ^ mask: swapped(part, mask) for slot, part in found.items()})
        return [found[slot] for slot in range(1, slots)]

    def alone(own):
        return [own] * (slots - 1)

    others = slots - 1
    received = lax.cond(lax.axis_index("ctx") < slots, gathered, alone, own_kv)
    later = (len(sends) - 1) * split
    more = call(
        functools.partial(later_load_kernel, sends[1:], split, heads, others),
        "later_load",
        [*cut_shapes(sends[1:]), shape(queries.shape[1:])] + [shape((tok_dev, 2 * wide))] * others,
        [spec(HBM)] * (2 + others),
        [spec()] * (later + 1 + others),
        scratch_shapes=[pltpu.SemaphoreType.DMA((later + 1 + others,))],
    )(up, own_queries, *(in_hbm(part) for part in received))
    own_queries, kv = more[later], [own_kv, *more[later + 1 :]]
    cut = [*cut, *more[:later]]
    pieces = [
        [across(cut[at * split + step], step) for step in range(split)] for at in range(len(sends))
    ]

    def pieces_of(first, count):
        return [piece for at in overlaps(sends, first, count) for piece in pieces[at]]

    ins = (own_queries, selected[0], *kv)
    weights, outs = call(
        functools.partial(weights_kernel, slots, heads),
        "weights",
        [shape((heads, slots * tok_dev, rows)), shape((tok_dev, heads * HEAD_COLS))],
        [spec()] * len(ins),
        [spec()] * 2,
    )(*ins)

    def sums_of(name, group, span, layout, grads=None, done=()):
        first, count = group
        used = pieces_of(first, count) if grads is None else [grads]
        before = done[0].shape[1] // (len(layout[0][2]) * HD) if done else 0
        ins = (weights, outs, own_queries, *kv[span[0] : span[1]], *done, *used)
        results = [shape((tok_dev, count * HEAD_COLS))] if grads is None else []
        results.append(shape((count, (span[1] - span[0]) * tok_dev, rows)))
        results.extend(
            shape(((to - at) * tok_dev, len(kinds) * (before + count) * HD), dtype)
            for at, to, kinds, dtype in layout
        )
        return call(
            functools.partial(
                sums_kernel,
                span,
                first,
                count,
                sends,
                0 if grads is not None else split,
                before,
                [part[:3] for part in layout],
            ),
            name,
            results,
            [spec()] * len(ins),
            [spec()] * len(results),
        )(*ins)

    def query_of(score_grads, places):
        ins = (*score_grads, *kv)
        return call(
            functools.partial(query_kernel, slots, places, len(score_grads)),
            "query",
            shape((tok_dev, heads * HEAD_COLS)),
            [spec()] * len(ins),
            spec(HBM),
            scratch_shapes=[
                pltpu.VMEM((tok_dev, heads * HEAD_COLS), BF16),
                pltpu.SemaphoreType.DMA((heads,)),
            ],
        )(*ins)

    def added(keep, received, outs, *after):
        ins = (keep, received, *after)
        return call(
            functools.partial(add_kernel, len(outs)), "add", outs, [spec()] * len(ins), [spec()] * len(outs)
        )(*ins)

    both = ("key", "value")
    if paired:
        _, scores_a, keep, send = sums_of("sums_early", (0, 2), (0, 4), [(0, 2, both, F32), (2, 4, both, BF16)])
        part = (tok_dev, 4 * HD)
        own, send = added(keep, swapped(send, 2), [shape(part, F32), shape(part)])
        found = [own, swapped(send, 1)]

        near = [(0, 1, both, F32), (1, 2, ("key",), BF16), (1, 2, ("value",), BF16)]
        kept, sent = (2, 3, both, F32), (3, 4, both, BF16)
        _, scores_b, *near_done, keep, send = sums_of("sums_middle", (2, 1), (0, 4), [*near, kept, sent])
        grads, scores_3, send = sums_of("sums_3", (3, 1), (3, 4), [sent], done=[send])
        scores_2, keep = sums_of("sums_2", (3, 1), (2, 3), [kept], grads, [keep])
        scores_01, own, *sends_1 = sums_of("sums_01", (3, 1), (0, 2), near, grads, near_done)
        (send,) = added(keep, swapped(send, 1), [shape(part)], own)
        query_grad = query_of(
            [scores_a, scores_b, scores_01, scores_2, scores_3],
            [((0,), 0), ((0,), 1), ((1,), 0), ((2, 3, 4), 0)],
        )
        found.extend([own, swapped(send, 2), *(swapped(part, 1) for part in sends_1)])
        counts = [(2, 0), (2, 1)]
    else:
        layout = [(0, 1, both, F32)] + [(slot, slot + 1, both, BF16) for slot in range(1, slots)]
        _, scores, own, *send = sums_of("sums", groups[0], (0, slots), layout)
        query_grad = query_of([scores], [((0,), head) for head in range(heads)])
        found = [own, *(swapped(part, slot) for slot, part in enumerate(send, 1))]
        counts = [(slots, 0)]

    key_grad, value_grad = call(
        functools.partial(finish_kernel, groups, counts),
        "finish",
        [shape((tok_dev, wide))] * 2,
        [spec()] * len(found),
        [spec()] * 2,
    )(*found)
    return query_grad[None], key_grad[None], value_grad[None]


def solution(mesh):
    split = P("pipe", "ctx", "head")
    placed = (split, split, split, P("pipe", ("ctx", "head"), None), P("pipe", "head", "ctx", None))
    return jax.shard_map(
        per_device, mesh=mesh, in_specs=placed, out_specs=(split, split, split), check_vma=False
    )
```

```python
import functools

import jax
import jax.numpy as jnp
from jax import lax
from jax.experimental import pallas as pl
from jax.experimental.pallas import tpu as pltpu
from jax.sharding import PartitionSpec as P

HD = 128
BLK = 64
GROUP = 8
HEAD_COLS = GROUP * HD
LOG2E = 1.4426950408889634
SCALE = HD**-0.5
VMEM = pltpu.MemorySpace.VMEM
HBM = pltpu.MemorySpace.HBM
BF16 = jnp.bfloat16
F32 = jnp.float32


def spec(space=VMEM):
    return pl.BlockSpec(memory_space=space)


def in_hbm(value):
    return pltpu.with_memory_space_constraint(value, HBM)


def shape(dims, dtype=BF16):
    return jax.ShapeDtypeStruct(dims, dtype)


def call(body, name, out_shape, in_specs, out_specs, **rest):
    return pl.pallas_call(
        body,
        out_shape=out_shape,
        in_specs=in_specs,
        out_specs=out_specs,
        name=name,
        cost_estimate=pl.CostEstimate(flops=1024, bytes_accessed=1024, transcendentals=0),
        compiler_params=pltpu.CompilerParams(vmem_limit_bytes=24 << 20),
        **rest,
    )


def contract(a, b, dims):
    return lax.dot_general(a, b, (dims, ((), ())), preferred_element_type=F32)


def head_rows(ref, head):
    first = head * HEAD_COLS
    return jnp.concatenate([ref[:, first + g * HD : first + (g + 1) * HD] for g in range(GROUP)], axis=0)


def key_rows(kv_refs, head):
    return jnp.concatenate([ref[:, head * HD : (head + 1) * HD] for ref in kv_refs], axis=0)


def value_rows(kv_refs, head):
    first = kv_refs[0].shape[1] // 2 + head * HD
    return jnp.concatenate([ref[:, first : first + HD] for ref in kv_refs], axis=0)


def store_rows(ref, column, turned):
    rows = ref.shape[0]
    for g in range(GROUP):
        ref[:, column + g * HD : column + (g + 1) * HD] = turned[:, g * rows : (g + 1) * rows].T


def run_copies(copies, sem):
    copies = [pltpu.make_async_copy(src, dst, sem.at[at]) for at, (src, dst) in enumerate(copies)]
    for copy in copies:
        copy.start()
    for copy in copies:
        copy.wait()


def cut_copies(sends, split, heads, up_ref, piece_refs):
    here = lax.axis_index("head")
    copies = []
    for at, (first, count) in enumerate(sends):
        for step in range(split):
            target = lax.rem(here + step, split)
            start = pl.multiple_of((target * heads * GROUP + first) * HD, HD)
            copies.append((up_ref.at[:, pl.ds(start, count * HD)], piece_refs[at * split + step]))
    return copies


def first_load_kernel(sends, split, heads, up_ref, k_ref, v_ref, *refs):
    *piece_refs, kv_out, sem = refs
    wide = k_ref.shape[1]
    copies = cut_copies(sends, split, heads, up_ref, piece_refs)
    run_copies([*copies, (k_ref, kv_out.at[:, :wide]), (v_ref, kv_out.at[:, wide:])], sem)


def later_load_kernel(sends, split, heads, others, up_ref, q_ref, *refs):
    other_refs, (*piece_refs, q_out), other_outs, sem = (
        refs[:others],
        refs[others : -1 - others],
        refs[-1 - others : -1],
        refs[-1],
    )
    copies = cut_copies(sends, split, heads, up_ref, piece_refs)
    run_copies([*copies, *zip(other_refs, other_outs), (q_ref, q_out)], sem)


def overlaps(sends, first, count):
    begin, end = first * GROUP, (first + count) * GROUP
    return [at for at, (start, size) in enumerate(sends) if start < end and start + size > begin]


def put_pieces(sends, first, split, grad_ref, piece_refs):
    here = lax.axis_index("head")
    begin, width = first * GROUP, grad_ref.shape[1] // HD
    for at, index in enumerate(overlaps(sends, first, width // GROUP)):
        start, size = sends[index]
        low, high = max(start, begin), min(start + size, begin + width)
        for step in range(split):
            piece = piece_refs[at * split + step]
            rows = piece.shape[0]
            source = lax.rem(here + split - step, split)
            grad_ref[
                pl.ds(pl.multiple_of(source * rows, rows), rows), (low - begin) * HD : (high - begin) * HD
            ] = piece[:, (low - start) * HD : (high - start) * HD]


def block_bias(slots, selected_ref, head, tok_dev):
    blocks = tok_dev // BLK
    here = lax.axis_index("ctx")
    at = lax.broadcasted_iota(jnp.int32, (slots * blocks, 1), 0)
    key_block = (here ^ (at // blocks)) * blocks + at % blocks
    columns = []
    for qb in range(blocks):
        hit = jnp.where(selected_ref[head, qb : qb + 1, :] == key_block, 1, 0)
        chosen = jnp.max(hit, axis=1, keepdims=True) > 0
        bias = jnp.where(chosen & (key_block <= here * blocks + qb), 0.0, -jnp.inf)
        columns.append(jnp.broadcast_to(bias, (slots * blocks, BLK)))
    return jnp.concatenate(columns * GROUP, axis=1)


def weights_kernel(slots, heads, q_ref, selected_ref, *refs):
    kv_refs, (p_ref, o_ref) = refs[:slots], refs[slots:]
    tok_dev = q_ref.shape[0]
    rows = GROUP * tok_dev
    key_at = lax.broadcasted_iota(jnp.int32, (tok_dev, rows), 0)
    query_at = lax.broadcasted_iota(jnp.int32, (tok_dev, rows), 1) % tok_dev
    causal = key_at <= query_at
    ahead = contract(key_rows(kv_refs, 0), head_rows(q_ref, 0), ((1,), (1,)))
    weights = None
    for head in range(heads + 1):
        scores = ahead
        if head + 1 < heads:
            ahead = contract(key_rows(kv_refs, head + 1), head_rows(q_ref, head + 1), ((1,), (1,)))
        before, weights = weights, None
        if head < heads:
            bias = block_bias(slots, selected_ref, head, tok_dev)
            scores = scores * (SCALE * LOG2E)
            parts = []
            for kb in range(slots * tok_dev // BLK):
                part = scores[kb * BLK : (kb + 1) * BLK] + bias[kb : kb + 1]
                if kb * BLK < tok_dev:
                    part = jnp.where(causal[kb * BLK : (kb + 1) * BLK], part, -jnp.inf)
                parts.append(part)
            scores = jnp.concatenate(parts, axis=0)
            shifted = jnp.exp2(scores - jnp.max(scores, axis=0, keepdims=True))
            weights = (shifted * (1.0 / jnp.sum(shifted, axis=0, keepdims=True))).astype(BF16)
            p_ref[head] = weights
        if before is not None:
            turned = contract(value_rows(kv_refs, head - 1).T, before, ((1,), (0,))).astype(BF16)
            store_rows(o_ref, (head - 1) * HEAD_COLS, turned)


def sums_kernel(slots, first, count, sends, split, before, layout, p_ref, o_ref, q_ref, *refs):
    begin, end = slots
    kv_refs, refs = refs[: end - begin], refs[end - begin :]
    if before:
        for ref, done_ref, (_, _, kinds) in zip(refs[-len(layout) :], refs, layout):
            for at in range(len(kinds)):
                to = at * (before + count) * HD
                ref[:, to : to + before * HD] = done_ref[:, at * before * HD : (at + 1) * before * HD]
        refs = refs[len(layout) :]
    if split:
        piece_refs = refs[: -2 - len(layout)]
        grad_ref, ds_ref, *sum_refs = refs[-2 - len(layout) :]
        put_pieces(sends, first, split, grad_ref, piece_refs)
        grads_of = [(grad_ref, local) for local in range(count)]
    else:
        ds_ref, *sum_refs = refs[-1 - len(layout) :]
        grads_of = [(ref, at) for ref in refs[: -1 - len(layout)] for at in range(ref.shape[1] // HEAD_COLS)]
    tok_dev = q_ref.shape[0]
    here = lax.axis_index("ctx")
    needed = functools.reduce(jnp.logical_or, [(here ^ slot) <= here for slot in range(begin, end)])

    @pl.when(needed)
    def work():
        for local in range(count):
            head = first + local
            grads, queries, outs = head_rows(*grads_of[local]), head_rows(q_ref, head), head_rows(o_ref, head)
            delta = (grads.astype(F32) * outs.astype(F32)).astype(BF16)
            weights = p_ref[head, begin * tok_dev : end * tok_dev]
            values = value_rows(kv_refs, head)
            left = jnp.concatenate([values, jnp.full(values.shape, -1, BF16)], axis=1)
            centred = contract(left, jnp.concatenate([grads, delta], axis=1), ((1,), (1,)))
            score_grad = (weights.astype(F32) * centred).astype(BF16)
            ds_ref[local] = score_grad
            sums = {
                "key": contract(score_grad, queries, ((1,), (0,))) * SCALE,
                "value": contract(weights, grads, ((1,), (0,))),
            }
            for ref, (from_slot, to_slot, kinds) in zip(sum_refs, layout):
                for at, kind in enumerate(kinds):
                    column = (at * (before + count) + before + local) * HD
                    part = sums[kind][(from_slot - begin) * tok_dev : (to_slot - begin) * tok_dev]
                    ref[:, column : column + HD] = part.astype(ref.dtype)

    @pl.when(jnp.logical_not(needed))
    def rest():
        ds_ref[...] = jnp.zeros_like(ds_ref)
        for ref in sum_refs:
            ref[...] = jnp.zeros_like(ref)


def query_kernel(slots, places, parts, *refs):
    ds_refs, kv_refs, (dq_ref, stage_ref, sem) = refs[:parts], refs[parts : parts + slots], refs[-3:]
    copies = []
    for head, place in enumerate(places):
        score_grad = jnp.concatenate([ds_refs[at][row] for at, row in place], axis=0)
        turned = (contract(key_rows(kv_refs, head).T, score_grad, ((1,), (0,))) * SCALE).astype(BF16)
        store_rows(stage_ref, head * HEAD_COLS, turned)
        columns = slice(head * HEAD_COLS, (head + 1) * HEAD_COLS)
        copies.append(
            pltpu.make_async_copy(stage_ref.at[:, columns], dq_ref.at[:, columns], sem.at[head])
        )
        copies[-1].start()
    for copy in copies:
        copy.wait()


def add_kernel(outs, keep_ref, received_ref, *refs):
    total = keep_ref[...] + received_ref[...].astype(F32)
    done = 0
    for ref in refs[-outs:]:
        ref[...] = total[done : done + ref.shape[0]].astype(ref.dtype)
        done += ref.shape[0]


def finish_kernel(groups, counts, *refs):
    key_ref, value_ref = refs[-2:]
    refs = list(refs[:-2])
    for (first, count), (whole, halves) in zip(groups, counts):
        parts, refs = refs[: whole + 2 * halves], refs[whole + 2 * halves :]
        width = count * HD
        keys = [ref[:, :width] for ref in parts[:whole]] + [ref[...] for ref in parts[whole::2]]
        values = [ref[:, width:] for ref in parts[:whole]] + [ref[...] for ref in parts[whole + 1 :: 2]]
        for ref, found in ((key_ref, keys), (value_ref, values)):
            total = sum(part.astype(F32) for part in found[1:]) + found[0]
            ref[:, first * HD : (first + count) * HD] = total.astype(BF16)


def per_device(queries, key_states, value_states, upstream, selected):
    slots = lax.axis_size("ctx")
    pipe, split = lax.axis_size("pipe"), lax.axis_size("head")
    tok_dev, rows_in = queries.shape[1], upstream.shape[1]
    heads = key_states.shape[2] // HD
    wide, rows = heads * HD, GROUP * tok_dev
    paired = heads == 4 and slots == 4
    groups = [(0, 2), (2, 2)] if paired else [(0, heads)]
    sends = [(0, 24), (24, 8)] if paired else [(0, heads * GROUP)]

    def swapped(value, mask):
        return lax.ppermute(value, "ctx", [(place, place ^ mask) for place in range(slots)])

    def across(part, step):
        route = [
            (sec * split + at, (sec - 1) % pipe * split + (at + step) % split)
            for sec in range(pipe)
            for at in range(split)
        ]
        return lax.ppermute(part, ("pipe", "head"), route)

    up, own_queries, own_keys, own_values = (
        in_hbm(value[0]) for value in (upstream, queries, key_states, value_states)
    )

    def cut_shapes(sends):
        return [shape((rows_in, count * HD)) for _, count in sends for _ in range(split)]

    *cut, own_kv = call(
        functools.partial(first_load_kernel, sends[:1], split, heads),
        "first_load",
        [*cut_shapes(sends[:1]), shape((tok_dev, 2 * wide))],
        [spec(HBM)] * 3,
        [spec()] * (split + 1),
        scratch_shapes=[pltpu.SemaphoreType.DMA((split + 2,))],
    )(up, own_keys, own_values)

    def gathered(own):
        found = {0: own}
        for mask in [1 << bit for bit in reversed(range(slots.bit_length() - 1))]:
            found.update({slot ^ mask: swapped(part, mask) for slot, part in found.items()})
        return [found[slot] for slot in range(1, slots)]

    def alone(own):
        return [own] * (slots - 1)

    others = slots - 1
    received = lax.cond(lax.axis_index("ctx") < slots, gathered, alone, own_kv)
    later = (len(sends) - 1) * split
    more = call(
        functools.partial(later_load_kernel, sends[1:], split, heads, others),
        "later_load",
        [*cut_shapes(sends[1:]), shape(queries.shape[1:])] + [shape((tok_dev, 2 * wide))] * others,
        [spec(HBM)] * (2 + others),
        [spec()] * (later + 1 + others),
        scratch_shapes=[pltpu.SemaphoreType.DMA((later + 1 + others,))],
    )(up, own_queries, *(in_hbm(part) for part in received))
    own_queries, kv = more[later], [own_kv, *more[later + 1 :]]
    cut = [*cut, *more[:later]]
    pieces = [
        [across(cut[at * split + step], step) for step in range(split)] for at in range(len(sends))
    ]

    def pieces_of(first, count):
        return [piece for at in overlaps(sends, first, count) for piece in pieces[at]]

    ins = (own_queries, selected[0], *kv)
    weights, outs = call(
        functools.partial(weights_kernel, slots, heads),
        "weights",
        [shape((heads, slots * tok_dev, rows)), shape((tok_dev, heads * HEAD_COLS))],
        [spec()] * len(ins),
        [spec()] * 2,
    )(*ins)

    def sums_of(name, group, span, layout, grads=None, done=(), after=()):
        first, count = group
        used = pieces_of(first, count) if grads is None else grads
        before = done[0].shape[1] // (len(layout[0][2]) * HD) if done else 0
        ins = (weights, outs, own_queries, *kv[span[0] : span[1]], *done, *used, *after)
        results = [shape((tok_dev, count * HEAD_COLS))] if grads is None else []
        results.append(shape((count, (span[1] - span[0]) * tok_dev, rows)))
        results.extend(
            shape(((to - at) * tok_dev, len(kinds) * (before + count) * HD), dtype)
            for at, to, kinds, dtype in layout
        )
        return call(
            functools.partial(
                sums_kernel,
                span,
                first,
                count,
                sends,
                0 if grads is not None else split,
                before,
                [part[:3] for part in layout],
            ),
            name,
            results,
            [spec()] * len(ins),
            [spec()] * len(results),
        )(*ins)

    def query_of(score_grads, places):
        ins = (*score_grads, *kv)
        return call(
            functools.partial(query_kernel, slots, places, len(score_grads)),
            "query",
            shape((tok_dev, heads * HEAD_COLS)),
            [spec()] * len(ins),
            spec(HBM),
            scratch_shapes=[
                pltpu.VMEM((tok_dev, heads * HEAD_COLS), BF16),
                pltpu.SemaphoreType.DMA((heads,)),
            ],
        )(*ins)

    def added(keep, received, outs, *after):
        ins = (keep, received, *after)
        return call(
            functools.partial(add_kernel, len(outs)), "add", outs, [spec()] * len(ins), [spec()] * len(outs)
        )(*ins)

    both = ("key", "value")
    if paired:
        _, scores_a, keep_a, send = sums_of(
            "sums_early", (0, 2), (0, 4), [(0, 2, both, F32), (2, 4, both, BF16)]
        )
        arrived = swapped(send, 2)

        near = [(0, 1, both, F32), (1, 2, ("key",), BF16), (1, 2, ("value",), BF16)]
        kept, sent = (2, 3, both, F32), (3, 4, both, BF16)
        grads_b, scores_b, keep, send = sums_of("sums_middle", (2, 1), (2, 4), [kept, sent])
        grads_c, scores_3, send = sums_of("sums_3", (3, 1), (3, 4), [sent], done=[send])
        scores_2, keep = sums_of("sums_2", (3, 1), (2, 3), [kept], [grads_c], [keep])
        part = (tok_dev, 4 * HD)
        (send,) = added(keep, swapped(send, 1), [shape(part)])
        scores_01, own, *sends_1 = sums_of(
            "sums_01", (2, 2), (0, 2), near, [grads_b, grads_c], after=[send]
        )
        query_grad = query_of(
            [scores_a, scores_b, scores_01, scores_2, scores_3],
            [((0, 0),), ((0, 1),), ((2, 0), (1, 0)), ((2, 1), (3, 0), (4, 0))],
        )
        own_a, send_a = added(keep_a, arrived, [shape(part, F32), shape(part)], own)
        found = [own_a, swapped(send_a, 1)]
        found.extend([own, swapped(send, 2), *(swapped(part, 1) for part in sends_1)])
        counts = [(2, 0), (2, 1)]
    else:
        layout = [(0, 1, both, F32)] + [(slot, slot + 1, both, BF16) for slot in range(1, slots)]
        _, scores, own, *send = sums_of("sums", groups[0], (0, slots), layout)
        query_grad = query_of([scores], [((0, head),) for head in range(heads)])
        found = [own, *(swapped(part, slot) for slot, part in enumerate(send, 1))]
        counts = [(slots, 0)]

    key_grad, value_grad = call(
        functools.partial(finish_kernel, groups, counts),
        "finish",
        [shape((tok_dev, wide))] * 2,
        [spec()] * len(found),
        [spec()] * 2,
    )(*found)
    return query_grad[None], key_grad[None], value_grad[None]


def solution(mesh):
    split = P("pipe", "ctx", "head")
    placed = (split, split, split, P("pipe", ("ctx", "head"), None), P("pipe", "head", "ctx", None))
    return jax.shard_map(
        per_device, mesh=mesh, in_specs=placed, out_specs=(split, split, split), check_vma=False
    )
```

```python
import functools

import jax
import jax.numpy as jnp
from jax import lax
from jax.experimental import pallas as pl
from jax.experimental.pallas import tpu as pltpu
from jax.sharding import PartitionSpec as P

HD = 128
BLK = 64
GROUP = 8
HEAD_COLS = GROUP * HD
LOG2E = 1.4426950408889634
SCALE = HD**-0.5
VMEM = pltpu.MemorySpace.VMEM
HBM = pltpu.MemorySpace.HBM
BF16 = jnp.bfloat16
F32 = jnp.float32


def spec(space=VMEM):
    return pl.BlockSpec(memory_space=space)


def in_hbm(value):
    return pltpu.with_memory_space_constraint(value, HBM)


def shape(dims, dtype=BF16):
    return jax.ShapeDtypeStruct(dims, dtype)


def call(body, name, out_shape, in_specs, out_specs, **rest):
    return pl.pallas_call(
        body,
        out_shape=out_shape,
        in_specs=in_specs,
        out_specs=out_specs,
        name=name,
        cost_estimate=pl.CostEstimate(flops=1024, bytes_accessed=1024, transcendentals=0),
        compiler_params=pltpu.CompilerParams(vmem_limit_bytes=24 << 20),
        **rest,
    )


def contract(a, b, dims):
    return lax.dot_general(a, b, (dims, ((), ())), preferred_element_type=F32)


def head_rows(ref, head):
    first = head * HEAD_COLS
    return jnp.concatenate([ref[:, first + g * HD : first + (g + 1) * HD] for g in range(GROUP)], axis=0)


def key_rows(kv_refs, head):
    return jnp.concatenate([ref[:, head * HD : (head + 1) * HD] for ref in kv_refs], axis=0)


def value_rows(kv_refs, head):
    first = kv_refs[0].shape[1] // 2 + head * HD
    return jnp.concatenate([ref[:, first : first + HD] for ref in kv_refs], axis=0)


def store_rows(ref, column, turned):
    rows = ref.shape[0]
    for g in range(GROUP):
        ref[:, column + g * HD : column + (g + 1) * HD] = turned[:, g * rows : (g + 1) * rows].T


def run_copies(copies, sem):
    copies = [pltpu.make_async_copy(src, dst, sem.at[at]) for at, (src, dst) in enumerate(copies)]
    for copy in copies:
        copy.start()
    for copy in copies:
        copy.wait()


def cut_copies(sends, split, heads, up_ref, piece_refs):
    here = lax.axis_index("head")
    copies = []
    for at, (first, count) in enumerate(sends):
        for step in range(split):
            target = lax.rem(here + step, split)
            start = pl.multiple_of((target * heads * GROUP + first) * HD, HD)
            copies.append((up_ref.at[:, pl.ds(start, count * HD)], piece_refs[at * split + step]))
    return copies


def first_load_kernel(sends, split, heads, up_ref, k_ref, v_ref, *refs):
    *piece_refs, kv_out, sem = refs
    wide = k_ref.shape[1]
    copies = cut_copies(sends, split, heads, up_ref, piece_refs)
    run_copies([*copies, (k_ref, kv_out.at[:, :wide]), (v_ref, kv_out.at[:, wide:])], sem)


def later_load_kernel(sends, split, heads, others, up_ref, q_ref, *refs):
    other_refs, (*piece_refs, q_out), other_outs, sem = (
        refs[:others],
        refs[others : -1 - others],
        refs[-1 - others : -1],
        refs[-1],
    )
    copies = cut_copies(sends, split, heads, up_ref, piece_refs)
    run_copies([*copies, *zip(other_refs, other_outs), (q_ref, q_out)], sem)


def overlaps(sends, first, count):
    begin, end = first * GROUP, (first + count) * GROUP
    return [at for at, (start, size) in enumerate(sends) if start < end and start + size > begin]


def put_pieces(sends, first, split, grad_ref, piece_refs):
    here = lax.axis_index("head")
    begin, width = first * GROUP, grad_ref.shape[1] // HD
    for at, index in enumerate(overlaps(sends, first, width // GROUP)):
        start, size = sends[index]
        low, high = max(start, begin), min(start + size, begin + width)
        for step in range(split):
            piece = piece_refs[at * split + step]
            rows = piece.shape[0]
            source = lax.rem(here + split - step, split)
            grad_ref[
                pl.ds(pl.multiple_of(source * rows, rows), rows), (low - begin) * HD : (high - begin) * HD
            ] = piece[:, (low - start) * HD : (high - start) * HD]


def block_bias(slots, selected_ref, head, tok_dev):
    blocks = tok_dev // BLK
    here = lax.axis_index("ctx")
    at = lax.broadcasted_iota(jnp.int32, (slots * blocks, 1), 0)
    key_block = (here ^ (at // blocks)) * blocks + at % blocks
    columns = []
    for qb in range(blocks):
        hit = jnp.where(selected_ref[head, qb : qb + 1, :] == key_block, 1, 0)
        chosen = jnp.max(hit, axis=1, keepdims=True) > 0
        bias = jnp.where(chosen & (key_block <= here * blocks + qb), 0.0, -jnp.inf)
        columns.append(jnp.broadcast_to(bias, (slots * blocks, BLK)))
    return jnp.concatenate(columns * GROUP, axis=1)


def weights_kernel(slots, heads, q_ref, selected_ref, *refs):
    kv_refs, (p_ref, o_ref) = refs[:slots], refs[slots:]
    tok_dev = q_ref.shape[0]
    rows = GROUP * tok_dev
    key_at = lax.broadcasted_iota(jnp.int32, (tok_dev, rows), 0)
    query_at = lax.broadcasted_iota(jnp.int32, (tok_dev, rows), 1) % tok_dev
    causal = key_at <= query_at
    ahead = contract(key_rows(kv_refs, 0), head_rows(q_ref, 0), ((1,), (1,)))
    weights = None
    for head in range(heads + 1):
        scores = ahead
        if head + 1 < heads:
            ahead = contract(key_rows(kv_refs, head + 1), head_rows(q_ref, head + 1), ((1,), (1,)))
        before, weights = weights, None
        if head < heads:
            bias = block_bias(slots, selected_ref, head, tok_dev)
            scores = scores * (SCALE * LOG2E)
            parts = []
            for kb in range(slots * tok_dev // BLK):
                part = scores[kb * BLK : (kb + 1) * BLK] + bias[kb : kb + 1]
                if kb * BLK < tok_dev:
                    part = jnp.where(causal[kb * BLK : (kb + 1) * BLK], part, -jnp.inf)
                parts.append(part)
            scores = jnp.concatenate(parts, axis=0)
            shifted = jnp.exp2(scores - jnp.max(scores, axis=0, keepdims=True))
            weights = (shifted * (1.0 / jnp.sum(shifted, axis=0, keepdims=True))).astype(BF16)
            p_ref[head] = weights
        if before is not None:
            values = value_rows(kv_refs, head - 1).T
            left = jnp.concatenate([values, jnp.ones((16, values.shape[1]), BF16)], axis=0)
            turned = contract(left, before, ((1,), (0,)))
            store_rows(o_ref, (head - 1) * HEAD_COLS, turned[:HD] * (1.0 / turned[HD : HD + 1]))


def in_parts(column):
    lane = lax.broadcasted_iota(jnp.int32, (column.shape[0], HD), 1)
    parts = jnp.zeros((column.shape[0], HD), F32)
    for at in range(3):
        part = column.astype(BF16).astype(F32)
        column = column - part
        parts = jnp.where(lane == at, part, parts)
    return parts.astype(BF16)


def sums_kernel(slots, first, count, sends, split, before, layout, p_ref, o_ref, q_ref, *refs):
    begin, end = slots
    kv_refs, refs = refs[: end - begin], refs[end - begin :]
    if before:
        for ref, done_ref, (_, _, kinds) in zip(refs[-len(layout) :], refs, layout):
            for at in range(len(kinds)):
                to = at * (before + count) * HD
                ref[:, to : to + before * HD] = done_ref[:, at * before * HD : (at + 1) * before * HD]
        refs = refs[len(layout) :]
    if split:
        piece_refs = refs[: -2 - len(layout)]
        grad_ref, ds_ref, *sum_refs = refs[-2 - len(layout) :]
        put_pieces(sends, first, split, grad_ref, piece_refs)
        grads_of = [(grad_ref, local) for local in range(count)]
    else:
        ds_ref, *sum_refs = refs[-1 - len(layout) :]
        grads_of = [(ref, at) for ref in refs[: -1 - len(layout)] for at in range(ref.shape[1] // HEAD_COLS)]
    tok_dev = q_ref.shape[0]
    here = lax.axis_index("ctx")
    needed = functools.reduce(jnp.logical_or, [(here ^ slot) <= here for slot in range(begin, end)])

    @pl.when(needed)
    def work():
        for local in range(count):
            head = first + local
            grads, queries, outs = head_rows(*grads_of[local]), head_rows(q_ref, head), head_rows(o_ref, head)
            delta = in_parts(jnp.sum(grads.astype(F32) * outs, axis=1, keepdims=True))
            weights = p_ref[head, begin * tok_dev : end * tok_dev]
            values = value_rows(kv_refs, head)
            left = jnp.concatenate([values, jnp.full(values.shape, -1, BF16)], axis=1)
            centred = contract(left, jnp.concatenate([grads, delta], axis=1), ((1,), (1,)))
            score_grad = (weights.astype(F32) * centred).astype(BF16)
            ds_ref[local] = score_grad
            sums = {
                "key": contract(score_grad, queries, ((1,), (0,))) * SCALE,
                "value": contract(weights, grads, ((1,), (0,))),
            }
            for ref, (from_slot, to_slot, kinds) in zip(sum_refs, layout):
                for at, kind in enumerate(kinds):
                    column = (at * (before + count) + before + local) * HD
                    part = sums[kind][(from_slot - begin) * tok_dev : (to_slot - begin) * tok_dev]
                    ref[:, column : column + HD] = part.astype(ref.dtype)

    @pl.when(jnp.logical_not(needed))
    def rest():
        ds_ref[...] = jnp.zeros_like(ds_ref)
        for ref in sum_refs:
            ref[...] = jnp.zeros_like(ref)


def query_kernel(slots, places, parts, *refs):
    ds_refs, kv_refs, (dq_ref, stage_ref, sem) = refs[:parts], refs[parts : parts + slots], refs[-3:]
    copies = []
    for head, place in enumerate(places):
        score_grad = jnp.concatenate([ds_refs[at][row] for at, row in place], axis=0)
        turned = (contract(key_rows(kv_refs, head).T, score_grad, ((1,), (0,))) * SCALE).astype(BF16)
        store_rows(stage_ref, head * HEAD_COLS, turned)
        columns = slice(head * HEAD_COLS, (head + 1) * HEAD_COLS)
        copies.append(
            pltpu.make_async_copy(stage_ref.at[:, columns], dq_ref.at[:, columns], sem.at[head])
        )
        copies[-1].start()
    for copy in copies:
        copy.wait()


def add_kernel(outs, keep_ref, received_ref, *refs):
    total = keep_ref[...] + received_ref[...].astype(F32)
    done = 0
    for ref in refs[-outs:]:
        ref[...] = total[done : done + ref.shape[0]].astype(ref.dtype)
        done += ref.shape[0]


def finish_kernel(groups, counts, *refs):
    key_ref, value_ref = refs[-2:]
    refs = list(refs[:-2])
    for (first, count), (whole, halves) in zip(groups, counts):
        parts, refs = refs[: whole + 2 * halves], refs[whole + 2 * halves :]
        width = count * HD
        keys = [ref[:, :width] for ref in parts[:whole]] + [ref[...] for ref in parts[whole::2]]
        values = [ref[:, width:] for ref in parts[:whole]] + [ref[...] for ref in parts[whole + 1 :: 2]]
        for ref, found in ((key_ref, keys), (value_ref, values)):
            total = sum(part.astype(F32) for part in found[1:]) + found[0]
            ref[:, first * HD : (first + count) * HD] = total.astype(BF16)


def per_device(queries, key_states, value_states, upstream, selected):
    slots = lax.axis_size("ctx")
    pipe, split = lax.axis_size("pipe"), lax.axis_size("head")
    tok_dev, rows_in = queries.shape[1], upstream.shape[1]
    heads = key_states.shape[2] // HD
    wide, rows = heads * HD, GROUP * tok_dev
    paired = heads == 4 and slots == 4
    groups = [(0, 2), (2, 2)] if paired else [(0, heads)]
    sends = [(0, 24), (24, 8)] if paired else [(0, heads * GROUP)]

    def swapped(value, mask):
        return lax.ppermute(value, "ctx", [(place, place ^ mask) for place in range(slots)])

    def across(part, step):
        route = [
            (sec * split + at, (sec - 1) % pipe * split + (at + step) % split)
            for sec in range(pipe)
            for at in range(split)
        ]
        return lax.ppermute(part, ("pipe", "head"), route)

    up, own_queries, own_keys, own_values = (
        in_hbm(value[0]) for value in (upstream, queries, key_states, value_states)
    )

    def cut_shapes(sends):
        return [shape((rows_in, count * HD)) for _, count in sends for _ in range(split)]

    *cut, own_kv = call(
        functools.partial(first_load_kernel, sends[:1], split, heads),
        "first_load",
        [*cut_shapes(sends[:1]), shape((tok_dev, 2 * wide))],
        [spec(HBM)] * 3,
        [spec()] * (split + 1),
        scratch_shapes=[pltpu.SemaphoreType.DMA((split + 2,))],
    )(up, own_keys, own_values)

    def gathered(own):
        found = {0: own}
        for mask in [1 << bit for bit in reversed(range(slots.bit_length() - 1))]:
            found.update({slot ^ mask: swapped(part, mask) for slot, part in found.items()})
        return [found[slot] for slot in range(1, slots)]

    def alone(own):
        return [own] * (slots - 1)

    others = slots - 1
    received = lax.cond(lax.axis_index("ctx") < slots, gathered, alone, own_kv)
    later = (len(sends) - 1) * split
    more = call(
        functools.partial(later_load_kernel, sends[1:], split, heads, others),
        "later_load",
        [*cut_shapes(sends[1:]), shape(queries.shape[1:])] + [shape((tok_dev, 2 * wide))] * others,
        [spec(HBM)] * (2 + others),
        [spec()] * (later + 1 + others),
        scratch_shapes=[pltpu.SemaphoreType.DMA((later + 1 + others,))],
    )(up, own_queries, *(in_hbm(part) for part in received))
    own_queries, kv = more[later], [own_kv, *more[later + 1 :]]
    cut = [*cut, *more[:later]]
    pieces = [
        [across(cut[at * split + step], step) for step in range(split)] for at in range(len(sends))
    ]

    def pieces_of(first, count):
        return [piece for at in overlaps(sends, first, count) for piece in pieces[at]]

    ins = (own_queries, selected[0], *kv)
    weights, outs = call(
        functools.partial(weights_kernel, slots, heads),
        "weights",
        [shape((heads, slots * tok_dev, rows)), shape((tok_dev, heads * HEAD_COLS), F32)],
        [spec()] * len(ins),
        [spec()] * 2,
    )(*ins)

    def sums_of(name, group, span, layout, grads=None, done=(), after=()):
        first, count = group
        used = pieces_of(first, count) if grads is None else grads
        before = done[0].shape[1] // (len(layout[0][2]) * HD) if done else 0
        ins = (weights, outs, own_queries, *kv[span[0] : span[1]], *done, *used, *after)
        results = [shape((tok_dev, count * HEAD_COLS))] if grads is None else []
        results.append(shape((count, (span[1] - span[0]) * tok_dev, rows)))
        results.extend(
            shape(((to - at) * tok_dev, len(kinds) * (before + count) * HD), dtype)
            for at, to, kinds, dtype in layout
        )
        return call(
            functools.partial(
                sums_kernel,
                span,
                first,
                count,
                sends,
                0 if grads is not None else split,
                before,
                [part[:3] for part in layout],
            ),
            name,
            results,
            [spec()] * len(ins),
            [spec()] * len(results),
        )(*ins)

    def query_of(score_grads, places):
        ins = (*score_grads, *kv)
        return call(
            functools.partial(query_kernel, slots, places, len(score_grads)),
            "query",
            shape((tok_dev, heads * HEAD_COLS)),
            [spec()] * len(ins),
            spec(HBM),
            scratch_shapes=[
                pltpu.VMEM((tok_dev, heads * HEAD_COLS), BF16),
                pltpu.SemaphoreType.DMA((heads,)),
            ],
        )(*ins)

    def added(keep, received, outs, *after):
        ins = (keep, received, *after)
        return call(
            functools.partial(add_kernel, len(outs)), "add", outs, [spec()] * len(ins), [spec()] * len(outs)
        )(*ins)

    both = ("key", "value")
    if paired:
        _, scores_a, keep_a, send = sums_of(
            "sums_early", (0, 2), (0, 4), [(0, 2, both, F32), (2, 4, both, BF16)]
        )
        arrived = swapped(send, 2)

        near = [(0, 1, both, F32), (1, 2, ("key",), BF16), (1, 2, ("value",), BF16)]
        kept, sent = (2, 3, both, F32), (3, 4, both, BF16)
        grads_b, scores_b, keep, send = sums_of("sums_middle", (2, 1), (2, 4), [kept, sent])
        grads_c, scores_3, send = sums_of("sums_3", (3, 1), (3, 4), [sent], done=[send])
        scores_2, keep = sums_of("sums_2", (3, 1), (2, 3), [kept], [grads_c], [keep])
        part = (tok_dev, 4 * HD)
        (send,) = added(keep, swapped(send, 1), [shape(part)])
        scores_01, own, *sends_1 = sums_of(
            "sums_01", (2, 2), (0, 2), near, [grads_b, grads_c], after=[send]
        )
        query_grad = query_of(
            [scores_a, scores_b, scores_01, scores_2, scores_3],
            [((0, 0),), ((0, 1),), ((2, 0), (1, 0)), ((2, 1), (3, 0), (4, 0))],
        )
        own_a, send_a = added(keep_a, arrived, [shape(part, F32), shape(part)], own)
        found = [own_a, swapped(send_a, 1)]
        found.extend([own, swapped(send, 2), *(swapped(part, 1) for part in sends_1)])
        counts = [(2, 0), (2, 1)]
    else:
        layout = [(0, 1, both, F32)] + [(slot, slot + 1, both, BF16) for slot in range(1, slots)]
        _, scores, own, *send = sums_of("sums", groups[0], (0, slots), layout)
        query_grad = query_of([scores], [((0, head),) for head in range(heads)])
        found = [own, *(swapped(part, slot) for slot, part in enumerate(send, 1))]
        counts = [(slots, 0)]

    key_grad, value_grad = call(
        functools.partial(finish_kernel, groups, counts),
        "finish",
        [shape((tok_dev, wide))] * 2,
        [spec()] * len(found),
        [spec()] * 2,
    )(*found)
    return query_grad[None], key_grad[None], value_grad[None]


def solution(mesh):
    split = P("pipe", "ctx", "head")
    placed = (split, split, split, P("pipe", ("ctx", "head"), None), P("pipe", "head", "ctx", None))
    return jax.shard_map(
        per_device, mesh=mesh, in_specs=placed, out_specs=(split, split, split), check_vma=False
    )
```

```python
import functools

import jax
import jax.numpy as jnp
from jax import lax
from jax.experimental import pallas as pl
from jax.experimental.pallas import tpu as pltpu
from jax.sharding import PartitionSpec as P

HD = 128
BLK = 64
GROUP = 8
HEAD_COLS = GROUP * HD
LOG2E = 1.4426950408889634
SCALE = HD**-0.5
VMEM = pltpu.MemorySpace.VMEM
HBM = pltpu.MemorySpace.HBM
BF16 = jnp.bfloat16
F32 = jnp.float32


def spec(space=VMEM):
    return pl.BlockSpec(memory_space=space)


def in_hbm(value):
    return pltpu.with_memory_space_constraint(value, HBM)


def shape(dims, dtype=BF16):
    return jax.ShapeDtypeStruct(dims, dtype)


def call(body, name, out_shape, in_specs, out_specs, **rest):
    return pl.pallas_call(
        body,
        out_shape=out_shape,
        in_specs=in_specs,
        out_specs=out_specs,
        name=name,
        cost_estimate=pl.CostEstimate(flops=1024, bytes_accessed=1024, transcendentals=0),
        compiler_params=pltpu.CompilerParams(vmem_limit_bytes=24 << 20),
        **rest,
    )


def contract(a, b, dims):
    return lax.dot_general(a, b, (dims, ((), ())), preferred_element_type=F32)


def head_rows(ref, head):
    first = head * HEAD_COLS
    return jnp.concatenate([ref[:, first + g * HD : first + (g + 1) * HD] for g in range(GROUP)], axis=0)


def key_rows(kv_refs, head):
    return jnp.concatenate([ref[:, head * HD : (head + 1) * HD] for ref in kv_refs], axis=0)


def value_rows(kv_refs, head):
    first = kv_refs[0].shape[1] // 2 + head * HD
    return jnp.concatenate([ref[:, first : first + HD] for ref in kv_refs], axis=0)


def store_rows(ref, column, turned):
    rows = ref.shape[0]
    for g in range(GROUP):
        ref[:, column + g * HD : column + (g + 1) * HD] = turned[:, g * rows : (g + 1) * rows].T


def run_copies(copies, sem):
    copies = [pltpu.make_async_copy(src, dst, sem.at[at]) for at, (src, dst) in enumerate(copies)]
    for copy in copies:
        copy.start()
    for copy in copies:
        copy.wait()


def cut_copies(sends, split, heads, up_ref, piece_refs):
    here = lax.axis_index("head")
    copies = []
    for at, (first, count) in enumerate(sends):
        for step in range(split):
            target = lax.rem(here + step, split)
            start = pl.multiple_of((target * heads * GROUP + first) * HD, HD)
            copies.append((up_ref.at[:, pl.ds(start, count * HD)], piece_refs[at * split + step]))
    return copies


def first_load_kernel(sends, split, heads, up_ref, k_ref, v_ref, *refs):
    *piece_refs, kv_out, sem = refs
    wide = k_ref.shape[1]
    copies = cut_copies(sends, split, heads, up_ref, piece_refs)
    run_copies([*copies, (k_ref, kv_out.at[:, :wide]), (v_ref, kv_out.at[:, wide:])], sem)


def later_load_kernel(sends, split, heads, others, up_ref, q_ref, *refs):
    other_refs, (*piece_refs, q_out), other_outs, sem = (
        refs[:others],
        refs[others : -1 - others],
        refs[-1 - others : -1],
        refs[-1],
    )
    copies = cut_copies(sends, split, heads, up_ref, piece_refs)
    run_copies([*copies, *zip(other_refs, other_outs), (q_ref, q_out)], sem)


def overlaps(sends, first, count):
    begin, end = first * GROUP, (first + count) * GROUP
    return [at for at, (start, size) in enumerate(sends) if start < end and start + size > begin]


def put_pieces(sends, first, split, grad_ref, piece_refs):
    here = lax.axis_index("head")
    begin, width = first * GROUP, grad_ref.shape[1] // HD
    for at, index in enumerate(overlaps(sends, first, width // GROUP)):
        start, size = sends[index]
        low, high = max(start, begin), min(start + size, begin + width)
        for step in range(split):
            piece = piece_refs[at * split + step]
            rows = piece.shape[0]
            source = lax.rem(here + split - step, split)
            grad_ref[
                pl.ds(pl.multiple_of(source * rows, rows), rows), (low - begin) * HD : (high - begin) * HD
            ] = piece[:, (low - start) * HD : (high - start) * HD]


def block_bias(slots, selected_ref, head, tok_dev):
    blocks = tok_dev // BLK
    here = lax.axis_index("ctx")
    at = lax.broadcasted_iota(jnp.int32, (slots * blocks, 1), 0)
    key_block = (here ^ (at // blocks)) * blocks + at % blocks
    columns = []
    for qb in range(blocks):
        hit = jnp.where(selected_ref[head, qb : qb + 1, :] == key_block, 1, 0)
        chosen = jnp.max(hit, axis=1, keepdims=True) > 0
        bias = jnp.where(chosen & (key_block <= here * blocks + qb), 0.0, -jnp.inf)
        columns.append(jnp.broadcast_to(bias, (slots * blocks, BLK)))
    return jnp.concatenate(columns * GROUP, axis=1)


def weights_kernel(slots, heads, q_ref, selected_ref, *refs):
    kv_refs, (p_ref, o_ref) = refs[:slots], refs[slots:]
    tok_dev = q_ref.shape[0]
    rows = GROUP * tok_dev
    key_at = lax.broadcasted_iota(jnp.int32, (tok_dev, rows), 0)
    query_at = lax.broadcasted_iota(jnp.int32, (tok_dev, rows), 1) % tok_dev
    causal = key_at <= query_at
    ahead = contract(key_rows(kv_refs, 0), head_rows(q_ref, 0), ((1,), (1,)))
    weights = None
    for head in range(heads + 1):
        scores = ahead
        if head + 1 < heads:
            ahead = contract(key_rows(kv_refs, head + 1), head_rows(q_ref, head + 1), ((1,), (1,)))
        before, weights = weights, None
        if head < heads:
            bias = block_bias(slots, selected_ref, head, tok_dev)
            scores = scores * (SCALE * LOG2E)
            parts = []
            for kb in range(slots * tok_dev // BLK):
                part = scores[kb * BLK : (kb + 1) * BLK] + bias[kb : kb + 1]
                if kb * BLK < tok_dev:
                    part = jnp.where(causal[kb * BLK : (kb + 1) * BLK], part, -jnp.inf)
                parts.append(part)
            scores = jnp.concatenate(parts, axis=0)
            shifted = jnp.exp2(scores - jnp.max(scores, axis=0, keepdims=True))
            weights = (shifted * (1.0 / jnp.sum(shifted, axis=0, keepdims=True))).astype(BF16)
            p_ref[head] = weights
        if before is not None:
            values = value_rows(kv_refs, head - 1).T
            left = jnp.concatenate([values, jnp.ones((16, values.shape[1]), BF16)], axis=0)
            turned = contract(left, before, ((1,), (0,)))
            store_rows(o_ref, (head - 1) * HEAD_COLS, turned[:HD] * (1.0 / turned[HD : HD + 1]))


def in_parts(column):
    lane = lax.broadcasted_iota(jnp.int32, (column.shape[0], HD), 1)
    parts = jnp.zeros((column.shape[0], HD), F32)
    for at in range(3):
        part = column.astype(BF16).astype(F32)
        column = column - part
        parts = jnp.where(lane == at, part, parts)
    return parts.astype(BF16)


def sums_kernel(slots, first, count, sends, split, before, layout, p_ref, o_ref, q_ref, *refs):
    begin, end = slots
    kv_refs, refs = refs[: end - begin], refs[end - begin :]
    if before:
        for ref, done_ref, (_, _, kinds) in zip(refs[-len(layout) :], refs, layout):
            for at in range(len(kinds)):
                to = at * (before + count) * HD
                ref[:, to : to + before * HD] = done_ref[:, at * before * HD : (at + 1) * before * HD]
        refs = refs[len(layout) :]
    if split:
        piece_refs = refs[: -2 - len(layout)]
        grad_ref, ds_ref, *sum_refs = refs[-2 - len(layout) :]
        put_pieces(sends, first, split, grad_ref, piece_refs)
        grads_of = [(grad_ref, local) for local in range(count)]
    else:
        ds_ref, *sum_refs = refs[-1 - len(layout) :]
        grads_of = [(ref, at) for ref in refs[: -1 - len(layout)] for at in range(ref.shape[1] // HEAD_COLS)]
    tok_dev = q_ref.shape[0]
    here = lax.axis_index("ctx")
    needed = functools.reduce(jnp.logical_or, [(here ^ slot) <= here for slot in range(begin, end)])

    @pl.when(needed)
    def work():
        for local in range(count):
            head = first + local
            grads, queries, outs = head_rows(*grads_of[local]), head_rows(q_ref, head), head_rows(o_ref, head)
            delta = in_parts(jnp.sum(grads.astype(F32) * outs, axis=1, keepdims=True))
            weights = p_ref[head, begin * tok_dev : end * tok_dev]
            values = value_rows(kv_refs, head)
            left = jnp.concatenate([values, jnp.full(values.shape, -1, BF16)], axis=1)
            centred = contract(left, jnp.concatenate([grads, delta], axis=1), ((1,), (1,)))
            score_grad = (weights.astype(F32) * centred).astype(BF16)
            ds_ref[local] = score_grad
            sums = {
                "key": contract(score_grad, queries, ((1,), (0,))) * SCALE,
                "value": contract(weights, grads, ((1,), (0,))),
            }
            for ref, (from_slot, to_slot, kinds) in zip(sum_refs, layout):
                for at, kind in enumerate(kinds):
                    column = (at * (before + count) + before + local) * HD
                    part = sums[kind][(from_slot - begin) * tok_dev : (to_slot - begin) * tok_dev]
                    ref[:, column : column + HD] = part.astype(ref.dtype)

    @pl.when(jnp.logical_not(needed))
    def rest():
        ds_ref[...] = jnp.zeros_like(ds_ref)
        for ref in sum_refs:
            ref[...] = jnp.zeros_like(ref)


def query_kernel(slots, places, parts, *refs):
    ds_refs, kv_refs, (dq_ref, stage_ref, sem) = refs[:parts], refs[parts : parts + slots], refs[-3:]
    copies = []
    for head, place in enumerate(places):
        score_grad = jnp.concatenate([ds_refs[at][row] for at, row in place], axis=0)
        turned = (contract(key_rows(kv_refs, head).T, score_grad, ((1,), (0,))) * SCALE).astype(BF16)
        store_rows(stage_ref, head * HEAD_COLS, turned)
        columns = slice(head * HEAD_COLS, (head + 1) * HEAD_COLS)
        copies.append(
            pltpu.make_async_copy(stage_ref.at[:, columns], dq_ref.at[:, columns], sem.at[head])
        )
        copies[-1].start()
    for copy in copies:
        copy.wait()


def add_kernel(outs, keep_ref, received_ref, *refs):
    total = keep_ref[...] + received_ref[...].astype(F32)
    done = 0
    for ref in refs[-outs:]:
        ref[...] = total[done : done + ref.shape[0]].astype(ref.dtype)
        done += ref.shape[0]


def finish_kernel(groups, counts, *refs):
    key_ref, value_ref = refs[-2:]
    refs = list(refs[:-2])
    for (first, count), (whole, halves) in zip(groups, counts):
        parts, refs = refs[: whole + 2 * halves], refs[whole + 2 * halves :]
        width = count * HD
        keys = [ref[:, :width] for ref in parts[:whole]] + [ref[...] for ref in parts[whole::2]]
        values = [ref[:, width:] for ref in parts[:whole]] + [ref[...] for ref in parts[whole + 1 :: 2]]
        for ref, found in ((key_ref, keys), (value_ref, values)):
            total = sum(part.astype(F32) for part in found[1:]) + found[0]
            ref[:, first * HD : (first + count) * HD] = total.astype(BF16)


def per_device(queries, key_states, value_states, upstream, selected):
    slots = lax.axis_size("ctx")
    pipe, split = lax.axis_size("pipe"), lax.axis_size("head")
    tok_dev, rows_in = queries.shape[1], upstream.shape[1]
    heads = key_states.shape[2] // HD
    wide, rows = heads * HD, GROUP * tok_dev
    paired = heads == 4 and slots == 4
    groups = [(0, 2), (2, 2)] if paired else [(0, heads)]
    sends = [(0, 24), (24, 8)] if paired else [(0, heads * GROUP)]

    def swapped(value, mask):
        return lax.ppermute(value, "ctx", [(place, place ^ mask) for place in range(slots)])

    def across(part, step):
        route = [
            (sec * split + at, (sec - 1) % pipe * split + (at + step) % split)
            for sec in range(pipe)
            for at in range(split)
        ]
        return lax.ppermute(part, ("pipe", "head"), route)

    up, own_queries, own_keys, own_values = (
        in_hbm(value[0]) for value in (upstream, queries, key_states, value_states)
    )

    def cut_shapes(sends):
        return [shape((rows_in, count * HD)) for _, count in sends for _ in range(split)]

    *cut, own_kv = call(
        functools.partial(first_load_kernel, sends[:1], split, heads),
        "first_load",
        [*cut_shapes(sends[:1]), shape((tok_dev, 2 * wide))],
        [spec(HBM)] * 3,
        [spec()] * (split + 1),
        scratch_shapes=[pltpu.SemaphoreType.DMA((split + 2,))],
    )(up, own_keys, own_values)

    def gathered(own):
        found = {0: own}
        for mask in [1 << bit for bit in reversed(range(slots.bit_length() - 1))]:
            found.update({slot ^ mask: swapped(part, mask) for slot, part in found.items()})
        return [found[slot] for slot in range(1, slots)]

    def alone(own):
        return [own] * (slots - 1)

    others = slots - 1
    received = lax.cond(lax.axis_index("ctx") < slots, gathered, alone, own_kv)
    later = (len(sends) - 1) * split
    more = call(
        functools.partial(later_load_kernel, sends[1:], split, heads, others),
        "later_load",
        [*cut_shapes(sends[1:]), shape(queries.shape[1:])] + [shape((tok_dev, 2 * wide))] * others,
        [spec(HBM)] * (2 + others),
        [spec()] * (later + 1 + others),
        scratch_shapes=[pltpu.SemaphoreType.DMA((later + 1 + others,))],
    )(up, own_queries, *(in_hbm(part) for part in received))
    own_queries, kv = more[later], [own_kv, *more[later + 1 :]]
    cut = [*cut, *more[:later]]
    pieces = [
        [across(cut[at * split + step], step) for step in range(split)] for at in range(len(sends))
    ]

    def pieces_of(first, count):
        return [piece for at in overlaps(sends, first, count) for piece in pieces[at]]

    ins = (own_queries, selected[0], *kv)
    weights, outs = call(
        functools.partial(weights_kernel, slots, heads),
        "weights",
        [shape((heads, slots * tok_dev, rows)), shape((tok_dev, heads * HEAD_COLS), F32)],
        [spec()] * len(ins),
        [spec()] * 2,
    )(*ins)

    def sums_of(name, group, span, layout, grads=None, done=(), after=()):
        first, count = group
        used = pieces_of(first, count) if grads is None else grads
        before = done[0].shape[1] // (len(layout[0][2]) * HD) if done else 0
        ins = (weights, outs, own_queries, *kv[span[0] : span[1]], *done, *used, *after)
        results = [shape((tok_dev, count * HEAD_COLS))] if grads is None else []
        results.append(shape((count, (span[1] - span[0]) * tok_dev, rows)))
        results.extend(
            shape(((to - at) * tok_dev, len(kinds) * (before + count) * HD), dtype)
            for at, to, kinds, dtype in layout
        )
        return call(
            functools.partial(
                sums_kernel,
                span,
                first,
                count,
                sends,
                0 if grads is not None else split,
                before,
                [part[:3] for part in layout],
            ),
            name,
            results,
            [spec()] * len(ins),
            [spec()] * len(results),
        )(*ins)

    def query_of(score_grads, places):
        ins = (*score_grads, *kv)
        return call(
            functools.partial(query_kernel, slots, places, len(score_grads)),
            "query",
            shape((tok_dev, heads * HEAD_COLS)),
            [spec()] * len(ins),
            spec(HBM),
            scratch_shapes=[
                pltpu.VMEM((tok_dev, heads * HEAD_COLS), BF16),
                pltpu.SemaphoreType.DMA((heads,)),
            ],
        )(*ins)

    def added(keep, received, outs, *after):
        ins = (keep, received, *after)
        return call(
            functools.partial(add_kernel, len(outs)), "add", outs, [spec()] * len(ins), [spec()] * len(outs)
        )(*ins)

    both = ("key", "value")
    if paired:
        _, scores_a, keep_a, send = sums_of(
            "sums_early", (0, 2), (0, 4), [(0, 2, both, F32), (2, 4, both, BF16)]
        )
        arrived = swapped(send, 2)

        near = [(0, 1, both, F32), (1, 2, ("key",), BF16), (1, 2, ("value",), BF16)]
        kept, sent = (2, 3, both, F32), (3, 4, both, BF16)
        _, scores_b, *near_done, keep, send = sums_of("sums_middle", (2, 1), (0, 4), [*near, kept, sent])
        grads_c, scores_3, send = sums_of("sums_3", (3, 1), (3, 4), [sent], done=[send])
        scores_2, keep = sums_of("sums_2", (3, 1), (2, 3), [kept], [grads_c], [keep])
        part = (tok_dev, 4 * HD)
        (send,) = added(keep, swapped(send, 1), [shape(part)])
        scores_01, own, *sends_1 = sums_of("sums_01", (3, 1), (0, 2), near, [grads_c], near_done, [send])
        query_grad = query_of(
            [scores_a, scores_b, scores_01, scores_2, scores_3],
            [((0, 0),), ((0, 1),), ((1, 0),), ((2, 0), (3, 0), (4, 0))],
        )
        own_a, send_a = added(keep_a, arrived, [shape(part, F32), shape(part)], own)
        found = [own_a, swapped(send_a, 1)]
        found.extend([own, swapped(send, 2), *(swapped(part, 1) for part in sends_1)])
        counts = [(2, 0), (2, 1)]
    else:
        layout = [(0, 1, both, F32)] + [(slot, slot + 1, both, BF16) for slot in range(1, slots)]
        _, scores, own, *send = sums_of("sums", groups[0], (0, slots), layout)
        query_grad = query_of([scores], [((0, head),) for head in range(heads)])
        found = [own, *(swapped(part, slot) for slot, part in enumerate(send, 1))]
        counts = [(slots, 0)]

    key_grad, value_grad = call(
        functools.partial(finish_kernel, groups, counts),
        "finish",
        [shape((tok_dev, wide))] * 2,
        [spec()] * len(found),
        [spec()] * 2,
    )(*found)
    return query_grad[None], key_grad[None], value_grad[None]


def solution(mesh):
    split = P("pipe", "ctx", "head")
    placed = (split, split, split, P("pipe", ("ctx", "head"), None), P("pipe", "head", "ctx", None))
    return jax.shard_map(
        per_device, mesh=mesh, in_specs=placed, out_specs=(split, split, split), check_vma=False
    )
```

```python
import functools

import jax
import jax.numpy as jnp
from jax import lax
from jax.experimental import pallas as pl
from jax.experimental.pallas import tpu as pltpu
from jax.sharding import PartitionSpec as P

HD = 128
BLK = 64
GROUP = 8
HEAD_COLS = GROUP * HD
LOG2E = 1.4426950408889634
SCALE = HD**-0.5
VMEM = pltpu.MemorySpace.VMEM
HBM = pltpu.MemorySpace.HBM
BF16 = jnp.bfloat16
F32 = jnp.float32


def spec(space=VMEM):
    return pl.BlockSpec(memory_space=space)


def in_hbm(value):
    return pltpu.with_memory_space_constraint(value, HBM)


def shape(dims, dtype=BF16):
    return jax.ShapeDtypeStruct(dims, dtype)


def call(body, name, out_shape, in_specs, out_specs, **rest):
    return pl.pallas_call(
        body,
        out_shape=out_shape,
        in_specs=in_specs,
        out_specs=out_specs,
        name=name,
        cost_estimate=pl.CostEstimate(flops=1024, bytes_accessed=1024, transcendentals=0),
        compiler_params=pltpu.CompilerParams(vmem_limit_bytes=24 << 20),
        **rest,
    )


def contract(a, b, dims):
    return lax.dot_general(a, b, (dims, ((), ())), preferred_element_type=F32)


def head_rows(ref, head):
    first = head * HEAD_COLS
    return jnp.concatenate([ref[:, first + g * HD : first + (g + 1) * HD] for g in range(GROUP)], axis=0)


def key_rows(kv_refs, head):
    return jnp.concatenate([ref[:, head * HD : (head + 1) * HD] for ref in kv_refs], axis=0)


def value_rows(kv_refs, head):
    first = kv_refs[0].shape[1] // 2 + head * HD
    return jnp.concatenate([ref[:, first : first + HD] for ref in kv_refs], axis=0)


def store_rows(ref, column, turned):
    rows = ref.shape[0]
    for g in range(GROUP):
        ref[:, column + g * HD : column + (g + 1) * HD] = turned[:, g * rows : (g + 1) * rows].T


def run_copies(copies, sem):
    copies = [pltpu.make_async_copy(src, dst, sem.at[at]) for at, (src, dst) in enumerate(copies)]
    for copy in copies:
        copy.start()
    for copy in copies:
        copy.wait()


def cut_copies(sends, split, heads, up_ref, piece_refs):
    here = lax.axis_index("head")
    copies = []
    for at, (first, count) in enumerate(sends):
        for step in range(split):
            target = lax.rem(here + step, split)
            start = pl.multiple_of((target * heads * GROUP + first) * HD, HD)
            copies.append((up_ref.at[:, pl.ds(start, count * HD)], piece_refs[at * split + step]))
    return copies


def first_load_kernel(sends, split, heads, up_ref, k_ref, v_ref, *refs):
    *piece_refs, kv_out, sem = refs
    wide = k_ref.shape[1]
    copies = cut_copies(sends, split, heads, up_ref, piece_refs)
    run_copies([*copies, (k_ref, kv_out.at[:, :wide]), (v_ref, kv_out.at[:, wide:])], sem)


def later_load_kernel(sends, split, heads, others, up_ref, q_ref, *refs):
    other_refs, (*piece_refs, q_out), other_outs, sem = (
        refs[:others],
        refs[others : -1 - others],
        refs[-1 - others : -1],
        refs[-1],
    )
    copies = cut_copies(sends, split, heads, up_ref, piece_refs)
    run_copies([*copies, *zip(other_refs, other_outs), (q_ref, q_out)], sem)


def overlaps(sends, first, count):
    begin, end = first * GROUP, (first + count) * GROUP
    return [at for at, (start, size) in enumerate(sends) if start < end and start + size > begin]


def put_pieces(sends, first, split, grad_ref, piece_refs):
    here = lax.axis_index("head")
    begin, width = first * GROUP, grad_ref.shape[1] // HD
    for at, index in enumerate(overlaps(sends, first, width // GROUP)):
        start, size = sends[index]
        low, high = max(start, begin), min(start + size, begin + width)
        for step in range(split):
            piece = piece_refs[at * split + step]
            rows = piece.shape[0]
            source = lax.rem(here + split - step, split)
            grad_ref[
                pl.ds(pl.multiple_of(source * rows, rows), rows), (low - begin) * HD : (high - begin) * HD
            ] = piece[:, (low - start) * HD : (high - start) * HD]


def block_bias(slots, selected_ref, head, tok_dev):
    blocks = tok_dev // BLK
    here = lax.axis_index("ctx")
    at = lax.broadcasted_iota(jnp.int32, (slots * blocks, 1), 0)
    key_block = (here ^ (at // blocks)) * blocks + at % blocks
    columns = []
    for qb in range(blocks):
        hit = jnp.where(selected_ref[head, qb : qb + 1, :] == key_block, 1, 0)
        chosen = jnp.max(hit, axis=1, keepdims=True) > 0
        bias = jnp.where(chosen & (key_block <= here * blocks + qb), 0.0, -jnp.inf)
        columns.append(jnp.broadcast_to(bias, (slots * blocks, BLK)))
    return jnp.concatenate(columns * GROUP, axis=1)


def weights_kernel(slots, heads, q_ref, selected_ref, *refs):
    kv_refs, (p_ref, o_ref) = refs[:slots], refs[slots:]
    tok_dev = q_ref.shape[0]
    rows = GROUP * tok_dev
    key_at = lax.broadcasted_iota(jnp.int32, (tok_dev, rows), 0)
    query_at = lax.broadcasted_iota(jnp.int32, (tok_dev, rows), 1) % tok_dev
    causal = key_at <= query_at
    ahead = contract(key_rows(kv_refs, 0), head_rows(q_ref, 0), ((1,), (1,)))
    weights = None
    for head in range(heads + 1):
        scores = ahead
        if head + 1 < heads:
            ahead = contract(key_rows(kv_refs, head + 1), head_rows(q_ref, head + 1), ((1,), (1,)))
        before, weights = weights, None
        if head < heads:
            bias = block_bias(slots, selected_ref, head, tok_dev)
            scores = scores * (SCALE * LOG2E)
            parts = []
            for kb in range(slots * tok_dev // BLK):
                part = scores[kb * BLK : (kb + 1) * BLK] + bias[kb : kb + 1]
                if kb * BLK < tok_dev:
                    part = jnp.where(causal[kb * BLK : (kb + 1) * BLK], part, -jnp.inf)
                parts.append(part)
            scores = jnp.concatenate(parts, axis=0)
            shifted = jnp.exp2(scores - jnp.max(scores, axis=0, keepdims=True))
            weights = (shifted * (1.0 / jnp.sum(shifted, axis=0, keepdims=True))).astype(BF16)
            p_ref[head] = weights
        if before is not None:
            values = value_rows(kv_refs, head - 1).T
            left = jnp.concatenate([values, jnp.ones((16, values.shape[1]), BF16)], axis=0)
            turned = contract(left, before, ((1,), (0,)))
            store_rows(o_ref, (head - 1) * HEAD_COLS, turned[:HD] * (1.0 / turned[HD : HD + 1]))


def in_parts(column):
    lane = lax.broadcasted_iota(jnp.int32, (column.shape[0], HD), 1)
    parts = jnp.zeros((column.shape[0], HD), F32)
    for at in range(3):
        part = column.astype(BF16).astype(F32)
        column = column - part
        parts = jnp.where(lane == at, part, parts)
    return parts.astype(BF16)


def sums_kernel(slots, first, count, sends, split, before, layout, p_ref, o_ref, q_ref, *refs):
    begin, end = slots
    kv_refs, refs = refs[: end - begin], refs[end - begin :]
    if before:
        for ref, done_ref, (_, _, kinds) in zip(refs[-len(layout) :], refs, layout):
            for at in range(len(kinds)):
                to = at * (before + count) * HD
                ref[:, to : to + before * HD] = done_ref[:, at * before * HD : (at + 1) * before * HD]
        refs = refs[len(layout) :]
    if split:
        piece_refs = refs[: -2 - len(layout)]
        grad_ref, ds_ref, *sum_refs = refs[-2 - len(layout) :]
        put_pieces(sends, first, split, grad_ref, piece_refs)
        grads_of = [(grad_ref, local) for local in range(count)]
    else:
        ds_ref, *sum_refs = refs[-1 - len(layout) :]
        grads_of = [(ref, at) for ref in refs[: -1 - len(layout)] for at in range(ref.shape[1] // HEAD_COLS)]
    tok_dev = q_ref.shape[0]
    here = lax.axis_index("ctx")
    needed = functools.reduce(jnp.logical_or, [(here ^ slot) <= here for slot in range(begin, end)])

    @pl.when(needed)
    def work():
        for local in range(count):
            head = first + local
            grads, queries, outs = head_rows(*grads_of[local]), head_rows(q_ref, head), head_rows(o_ref, head)
            delta = in_parts(jnp.sum(grads.astype(F32) * outs, axis=1, keepdims=True))
            weights = p_ref[head, begin * tok_dev : end * tok_dev]
            values = value_rows(kv_refs, head)
            left = jnp.concatenate([values, jnp.full(values.shape, -1, BF16)], axis=1)
            centred = contract(left, jnp.concatenate([grads, delta], axis=1), ((1,), (1,)))
            score_grad = (weights.astype(F32) * centred).astype(BF16)
            ds_ref[local] = score_grad
            sums = {
                "key": contract(score_grad, queries, ((1,), (0,))) * SCALE,
                "value": contract(weights, grads, ((1,), (0,))),
            }
            for ref, (from_slot, to_slot, kinds) in zip(sum_refs, layout):
                for at, kind in enumerate(kinds):
                    column = (at * (before + count) + before + local) * HD
                    part = sums[kind][(from_slot - begin) * tok_dev : (to_slot - begin) * tok_dev]
                    ref[:, column : column + HD] = part.astype(ref.dtype)

    @pl.when(jnp.logical_not(needed))
    def rest():
        ds_ref[...] = jnp.zeros_like(ds_ref)
        for ref in sum_refs:
            ref[...] = jnp.zeros_like(ref)


def query_kernel(slots, places, parts, *refs):
    ds_refs, kv_refs, (dq_ref, stage_ref, sem) = refs[:parts], refs[parts : parts + slots], refs[-3:]
    copies = []
    for head, place in enumerate(places):
        score_grad = jnp.concatenate([ds_refs[at][row] for at, row in place], axis=0)
        turned = (contract(key_rows(kv_refs, head).T, score_grad, ((1,), (0,))) * SCALE).astype(BF16)
        store_rows(stage_ref, head * HEAD_COLS, turned)
        columns = slice(head * HEAD_COLS, (head + 1) * HEAD_COLS)
        copies.append(
            pltpu.make_async_copy(stage_ref.at[:, columns], dq_ref.at[:, columns], sem.at[head])
        )
        copies[-1].start()
    for copy in copies:
        copy.wait()


def add_kernel(outs, keep_ref, received_ref, *refs):
    total = keep_ref[...] + received_ref[...].astype(F32)
    done = 0
    for ref in refs[-outs:]:
        ref[...] = total[done : done + ref.shape[0]].astype(ref.dtype)
        done += ref.shape[0]


def finish_kernel(groups, counts, *refs):
    key_ref, value_ref = refs[-2:]
    refs = list(refs[:-2])
    for (first, count), (whole, halves) in zip(groups, counts):
        parts, refs = refs[: whole + 2 * halves], refs[whole + 2 * halves :]
        width = count * HD
        keys = [ref[:, :width] for ref in parts[:whole]] + [ref[...] for ref in parts[whole::2]]
        values = [ref[:, width:] for ref in parts[:whole]] + [ref[...] for ref in parts[whole + 1 :: 2]]
        for ref, found in ((key_ref, keys), (value_ref, values)):
            total = sum(part.astype(F32) for part in found[1:]) + found[0]
            ref[:, first * HD : (first + count) * HD] = total.astype(BF16)


def per_device(queries, key_states, value_states, upstream, selected):
    slots = lax.axis_size("ctx")
    pipe, split = lax.axis_size("pipe"), lax.axis_size("head")
    tok_dev, rows_in = queries.shape[1], upstream.shape[1]
    heads = key_states.shape[2] // HD
    wide, rows = heads * HD, GROUP * tok_dev
    paired = heads == 4 and slots == 4
    groups = [(0, 2), (2, 2)] if paired else [(0, heads)]
    sends = [(0, 24), (24, 8)] if paired else [(0, heads * GROUP)]

    def swapped(value, mask):
        return lax.ppermute(value, "ctx", [(place, place ^ mask) for place in range(slots)])

    def across(part, step):
        route = [
            (sec * split + at, (sec - 1) % pipe * split + (at + step) % split)
            for sec in range(pipe)
            for at in range(split)
        ]
        return lax.ppermute(part, ("pipe", "head"), route)

    up, own_queries, own_keys, own_values = (
        in_hbm(value[0]) for value in (upstream, queries, key_states, value_states)
    )

    def cut_shapes(sends):
        return [shape((rows_in, count * HD)) for _, count in sends for _ in range(split)]

    *cut, own_kv = call(
        functools.partial(first_load_kernel, sends[:1], split, heads),
        "first_load",
        [*cut_shapes(sends[:1]), shape((tok_dev, 2 * wide))],
        [spec(HBM)] * 3,
        [spec()] * (split + 1),
        scratch_shapes=[pltpu.SemaphoreType.DMA((split + 2,))],
    )(up, own_keys, own_values)

    def gathered(own):
        found = {0: own}
        for mask in [1 << bit for bit in reversed(range(slots.bit_length() - 1))]:
            found.update({slot ^ mask: swapped(part, mask) for slot, part in found.items()})
        return [found[slot] for slot in range(1, slots)]

    def alone(own):
        return [own] * (slots - 1)

    others = slots - 1
    received = lax.cond(lax.axis_index("ctx") < slots, gathered, alone, own_kv)
    later = (len(sends) - 1) * split
    more = call(
        functools.partial(later_load_kernel, sends[1:], split, heads, others),
        "later_load",
        [*cut_shapes(sends[1:]), shape(queries.shape[1:])] + [shape((tok_dev, 2 * wide))] * others,
        [spec(HBM)] * (2 + others),
        [spec()] * (later + 1 + others),
        scratch_shapes=[pltpu.SemaphoreType.DMA((later + 1 + others,))],
    )(up, own_queries, *(in_hbm(part) for part in received))
    own_queries, kv = more[later], [own_kv, *more[later + 1 :]]
    cut = [*cut, *more[:later]]
    pieces = [
        [across(cut[at * split + step], step) for step in range(split)] for at in range(len(sends))
    ]

    def pieces_of(first, count):
        return [piece for at in overlaps(sends, first, count) for piece in pieces[at]]

    ins = (own_queries, selected[0], *kv)
    weights, outs = call(
        functools.partial(weights_kernel, slots, heads),
        "weights",
        [shape((heads, slots * tok_dev, rows)), shape((tok_dev, heads * HEAD_COLS), F32)],
        [spec()] * len(ins),
        [spec()] * 2,
    )(*ins)

    def sums_of(name, group, span, layout, grads=None, done=(), after=()):
        first, count = group
        used = pieces_of(first, count) if grads is None else grads
        before = done[0].shape[1] // (len(layout[0][2]) * HD) if done else 0
        ins = (weights, outs, own_queries, *kv[span[0] : span[1]], *done, *used, *after)
        results = [shape((tok_dev, count * HEAD_COLS))] if grads is None else []
        results.append(shape((count, (span[1] - span[0]) * tok_dev, rows)))
        results.extend(
            shape(((to - at) * tok_dev, len(kinds) * (before + count) * HD), dtype)
            for at, to, kinds, dtype in layout
        )
        return call(
            functools.partial(
                sums_kernel,
                span,
                first,
                count,
                sends,
                0 if grads is not None else split,
                before,
                [part[:3] for part in layout],
            ),
            name,
            results,
            [spec()] * len(ins),
            [spec()] * len(results),
        )(*ins)

    def query_of(score_grads, places):
        ins = (*score_grads, *kv)
        return call(
            functools.partial(query_kernel, slots, places, len(score_grads)),
            "query",
            shape((tok_dev, heads * HEAD_COLS)),
            [spec()] * len(ins),
            spec(HBM),
            scratch_shapes=[
                pltpu.VMEM((tok_dev, heads * HEAD_COLS), BF16),
                pltpu.SemaphoreType.DMA((heads,)),
            ],
        )(*ins)

    def added(keep, received, outs, *after):
        ins = (keep, received, *after)
        return call(
            functools.partial(add_kernel, len(outs)), "add", outs, [spec()] * len(ins), [spec()] * len(outs)
        )(*ins)

    both = ("key", "value")
    if paired:
        _, scores_a, keep_a, send = sums_of(
            "sums_early", (0, 2), (0, 4), [(0, 2, both, F32), (2, 4, both, BF16)]
        )
        arrived = swapped(send, 2)

        near = [(0, 1, both, F32), (1, 2, both, BF16)]
        kept, sent = (2, 3, both, F32), (3, 4, both, BF16)
        _, scores_b, *near_done, keep, send = sums_of("sums_middle", (2, 1), (0, 4), [*near, kept, sent])
        grads_c, scores_3, send = sums_of("sums_3", (3, 1), (3, 4), [sent], done=[send])
        scores_2, keep = sums_of("sums_2", (3, 1), (2, 3), [kept], [grads_c], [keep])
        part = (tok_dev, 4 * HD)
        (send,) = added(keep, swapped(send, 1), [shape(part)])
        scores_01, own, *sends_1 = sums_of("sums_01", (3, 1), (0, 2), near, [grads_c], near_done, [send])
        query_grad = query_of(
            [scores_a, scores_b, scores_01, scores_2, scores_3],
            [((0, 0),), ((0, 1),), ((1, 0),), ((2, 0), (3, 0), (4, 0))],
        )
        own_a, send_a = added(keep_a, arrived, [shape(part, F32), shape(part)], own)
        found = [own_a, swapped(send_a, 1)]
        found.extend([own, swapped(send, 2), *(swapped(part, 1) for part in sends_1)])
        counts = [(2, 0), (3, 0)]
    else:
        layout = [(0, 1, both, F32)] + [(slot, slot + 1, both, BF16) for slot in range(1, slots)]
        _, scores, own, *send = sums_of("sums", groups[0], (0, slots), layout)
        query_grad = query_of([scores], [((0, head),) for head in range(heads)])
        found = [own, *(swapped(part, slot) for slot, part in enumerate(send, 1))]
        counts = [(slots, 0)]

    key_grad, value_grad = call(
        functools.partial(finish_kernel, groups, counts),
        "finish",
        [shape((tok_dev, wide))] * 2,
        [spec()] * len(found),
        [spec()] * 2,
    )(*found)
    return query_grad[None], key_grad[None], value_grad[None]


def solution(mesh):
    split = P("pipe", "ctx", "head")
    placed = (split, split, split, P("pipe", ("ctx", "head"), None), P("pipe", "head", "ctx", None))
    return jax.shard_map(
        per_device, mesh=mesh, in_specs=placed, out_specs=(split, split, split), check_vma=False
    )
```

```python
import functools

import jax
import jax.numpy as jnp
from jax import lax
from jax.experimental import pallas as pl
from jax.experimental.pallas import tpu as pltpu
from jax.sharding import PartitionSpec as P

HD = 128
BLK = 64
GROUP = 8
HEAD_COLS = GROUP * HD
LOG2E = 1.4426950408889634
SCALE = HD**-0.5
VMEM = pltpu.MemorySpace.VMEM
HBM = pltpu.MemorySpace.HBM
BF16 = jnp.bfloat16
F32 = jnp.float32


def spec(space=VMEM):
    return pl.BlockSpec(memory_space=space)


def in_hbm(value):
    return pltpu.with_memory_space_constraint(value, HBM)


def shape(dims, dtype=BF16):
    return jax.ShapeDtypeStruct(dims, dtype)


def call(body, name, out_shape, in_specs, out_specs, **rest):
    return pl.pallas_call(
        body,
        out_shape=out_shape,
        in_specs=in_specs,
        out_specs=out_specs,
        name=name,
        cost_estimate=pl.CostEstimate(flops=1024, bytes_accessed=1024, transcendentals=0),
        compiler_params=pltpu.CompilerParams(vmem_limit_bytes=24 << 20),
        **rest,
    )


def contract(a, b, dims):
    return lax.dot_general(a, b, (dims, ((), ())), preferred_element_type=F32)


def head_rows(ref, head):
    first = head * HEAD_COLS
    return jnp.concatenate([ref[:, first + g * HD : first + (g + 1) * HD] for g in range(GROUP)], axis=0)


def key_rows(kv_refs, head):
    return jnp.concatenate([ref[:, head * HD : (head + 1) * HD] for ref in kv_refs], axis=0)


def value_rows(kv_refs, head):
    first = kv_refs[0].shape[1] // 2 + head * HD
    return jnp.concatenate([ref[:, first : first + HD] for ref in kv_refs], axis=0)


def store_rows(ref, column, turned):
    rows = ref.shape[0]
    for g in range(GROUP):
        ref[:, column + g * HD : column + (g + 1) * HD] = turned[:, g * rows : (g + 1) * rows].T


def run_copies(copies, sem):
    copies = [pltpu.make_async_copy(src, dst, sem.at[at]) for at, (src, dst) in enumerate(copies)]
    for copy in copies:
        copy.start()
    for copy in copies:
        copy.wait()


def cut_copies(sends, split, heads, up_ref, piece_refs):
    here = lax.axis_index("head")
    copies = []
    for at, (first, count) in enumerate(sends):
        for step in range(split):
            target = lax.rem(here + step, split)
            start = pl.multiple_of((target * heads * GROUP + first) * HD, HD)
            copies.append((up_ref.at[:, pl.ds(start, count * HD)], piece_refs[at * split + step]))
    return copies


def first_load_kernel(sends, split, heads, up_ref, k_ref, v_ref, *refs):
    *piece_refs, kv_out, sem = refs
    wide = k_ref.shape[1]
    copies = cut_copies(sends, split, heads, up_ref, piece_refs)
    run_copies([*copies, (k_ref, kv_out.at[:, :wide]), (v_ref, kv_out.at[:, wide:])], sem)


def later_load_kernel(sends, split, heads, others, up_ref, q_ref, *refs):
    other_refs, (*piece_refs, q_out), other_outs, sem = (
        refs[:others],
        refs[others : -1 - others],
        refs[-1 - others : -1],
        refs[-1],
    )
    copies = cut_copies(sends, split, heads, up_ref, piece_refs)
    run_copies([(q_ref, q_out), *zip(other_refs, other_outs), *copies], sem)


def overlaps(sends, first, count):
    begin, end = first * GROUP, (first + count) * GROUP
    return [at for at, (start, size) in enumerate(sends) if start < end and start + size > begin]


def put_pieces(sends, first, split, grad_ref, piece_refs):
    here = lax.axis_index("head")
    begin, width = first * GROUP, grad_ref.shape[1] // HD
    for at, index in enumerate(overlaps(sends, first, width // GROUP)):
        start, size = sends[index]
        low, high = max(start, begin), min(start + size, begin + width)
        for step in range(split):
            piece = piece_refs[at * split + step]
            rows = piece.shape[0]
            source = lax.rem(here + split - step, split)
            grad_ref[
                pl.ds(pl.multiple_of(source * rows, rows), rows), (low - begin) * HD : (high - begin) * HD
            ] = piece[:, (low - start) * HD : (high - start) * HD]


def block_bias(slots, selected_ref, head, tok_dev):
    blocks = tok_dev // BLK
    here = lax.axis_index("ctx")
    at = lax.broadcasted_iota(jnp.int32, (slots * blocks, 1), 0)
    key_block = (here ^ (at // blocks)) * blocks + at % blocks
    columns = []
    for qb in range(blocks):
        hit = jnp.where(selected_ref[head, qb : qb + 1, :] == key_block, 1, 0)
        chosen = jnp.max(hit, axis=1, keepdims=True) > 0
        bias = jnp.where(chosen & (key_block <= here * blocks + qb), 0.0, -jnp.inf)
        columns.append(jnp.broadcast_to(bias, (slots * blocks, BLK)))
    return jnp.concatenate(columns * GROUP, axis=1)


def weights_kernel(slots, heads, q_ref, selected_ref, *refs):
    kv_refs, (p_ref, o_ref) = refs[:slots], refs[slots:]
    tok_dev = q_ref.shape[0]
    rows = GROUP * tok_dev
    key_at = lax.broadcasted_iota(jnp.int32, (tok_dev, rows), 0)
    query_at = lax.broadcasted_iota(jnp.int32, (tok_dev, rows), 1) % tok_dev
    causal = key_at <= query_at
    ahead = contract(key_rows(kv_refs, 0), head_rows(q_ref, 0), ((1,), (1,)))
    weights = None
    for head in range(heads + 1):
        scores = ahead
        if head + 1 < heads:
            ahead = contract(key_rows(kv_refs, head + 1), head_rows(q_ref, head + 1), ((1,), (1,)))
        before, weights = weights, None
        if head < heads:
            bias = block_bias(slots, selected_ref, head, tok_dev)
            scores = scores * (SCALE * LOG2E)
            parts = []
            for kb in range(slots * tok_dev // BLK):
                part = scores[kb * BLK : (kb + 1) * BLK] + bias[kb : kb + 1]
                if kb * BLK < tok_dev:
                    part = jnp.where(causal[kb * BLK : (kb + 1) * BLK], part, -jnp.inf)
                parts.append(part)
            scores = jnp.concatenate(parts, axis=0)
            shifted = jnp.exp2(scores - jnp.max(scores, axis=0, keepdims=True))
            weights = (shifted * (1.0 / jnp.sum(shifted, axis=0, keepdims=True))).astype(BF16)
            p_ref[head] = weights
        if before is not None:
            values = value_rows(kv_refs, head - 1).T
            left = jnp.concatenate([values, jnp.ones((16, values.shape[1]), BF16)], axis=0)
            turned = contract(left, before, ((1,), (0,)))
            store_rows(o_ref, (head - 1) * HEAD_COLS, turned[:HD] * (1.0 / turned[HD : HD + 1]))


def in_parts(column):
    lane = lax.broadcasted_iota(jnp.int32, (column.shape[0], HD), 1)
    parts = jnp.zeros((column.shape[0], HD), F32)
    for at in range(3):
        part = column.astype(BF16).astype(F32)
        column = column - part
        parts = jnp.where(lane == at, part, parts)
    return parts.astype(BF16)


def sums_kernel(slots, first, count, sends, split, before, layout, p_ref, o_ref, q_ref, *refs):
    begin, end = slots
    kv_refs, refs = refs[: end - begin], refs[end - begin :]
    if before:
        for ref, done_ref, (_, _, kinds) in zip(refs[-len(layout) :], refs, layout):
            for at in range(len(kinds)):
                to = at * (before + count) * HD
                ref[:, to : to + before * HD] = done_ref[:, at * before * HD : (at + 1) * before * HD]
        refs = refs[len(layout) :]
    if split:
        piece_refs = refs[: -2 - len(layout)]
        grad_ref, ds_ref, *sum_refs = refs[-2 - len(layout) :]
        put_pieces(sends, first, split, grad_ref, piece_refs)
        grads_of = [(grad_ref, local) for local in range(count)]
    else:
        ds_ref, *sum_refs = refs[-1 - len(layout) :]
        grads_of = [(ref, at) for ref in refs[: -1 - len(layout)] for at in range(ref.shape[1] // HEAD_COLS)]
    tok_dev = q_ref.shape[0]
    here = lax.axis_index("ctx")
    needed = functools.reduce(jnp.logical_or, [(here ^ slot) <= here for slot in range(begin, end)])

    @pl.when(needed)
    def work():
        for local in range(count):
            head = first + local
            grads, queries, outs = head_rows(*grads_of[local]), head_rows(q_ref, head), head_rows(o_ref, head)
            delta = in_parts(jnp.sum(grads.astype(F32) * outs, axis=1, keepdims=True))
            weights = p_ref[head, begin * tok_dev : end * tok_dev]
            values = value_rows(kv_refs, head)
            left = jnp.concatenate([values, jnp.full(values.shape, -1, BF16)], axis=1)
            centred = contract(left, jnp.concatenate([grads, delta], axis=1), ((1,), (1,)))
            score_grad = (weights.astype(F32) * centred).astype(BF16)
            ds_ref[local] = score_grad
            sums = {
                "key": contract(score_grad, queries, ((1,), (0,))) * SCALE,
                "value": contract(weights, grads, ((1,), (0,))),
            }
            for ref, (from_slot, to_slot, kinds) in zip(sum_refs, layout):
                for at, kind in enumerate(kinds):
                    column = (at * (before + count) + before + local) * HD
                    part = sums[kind][(from_slot - begin) * tok_dev : (to_slot - begin) * tok_dev]
                    ref[:, column : column + HD] = part.astype(ref.dtype)

    @pl.when(jnp.logical_not(needed))
    def rest():
        ds_ref[...] = jnp.zeros_like(ds_ref)
        for ref in sum_refs:
            ref[...] = jnp.zeros_like(ref)


def query_kernel(slots, places, parts, *refs):
    ds_refs, kv_refs, (dq_ref, stage_ref, sem) = refs[:parts], refs[parts : parts + slots], refs[-3:]
    copies = []
    for head, place in enumerate(places):
        score_grad = jnp.concatenate([ds_refs[at][row] for at, row in place], axis=0)
        turned = (contract(key_rows(kv_refs, head).T, score_grad, ((1,), (0,))) * SCALE).astype(BF16)
        store_rows(stage_ref, head * HEAD_COLS, turned)
        columns = slice(head * HEAD_COLS, (head + 1) * HEAD_COLS)
        copies.append(
            pltpu.make_async_copy(stage_ref.at[:, columns], dq_ref.at[:, columns], sem.at[head])
        )
        copies[-1].start()
    for copy in copies:
        copy.wait()


def add_kernel(outs, keep_ref, received_ref, *refs):
    total = keep_ref[...] + received_ref[...].astype(F32)
    done = 0
    for ref in refs[-outs:]:
        ref[...] = total[done : done + ref.shape[0]].astype(ref.dtype)
        done += ref.shape[0]


def finish_kernel(groups, counts, *refs):
    key_ref, value_ref = refs[-2:]
    refs = list(refs[:-2])
    for (first, count), (whole, halves) in zip(groups, counts):
        parts, refs = refs[: whole + 2 * halves], refs[whole + 2 * halves :]
        width = count * HD
        keys = [ref[:, :width] for ref in parts[:whole]] + [ref[...] for ref in parts[whole::2]]
        values = [ref[:, width:] for ref in parts[:whole]] + [ref[...] for ref in parts[whole + 1 :: 2]]
        for ref, found in ((key_ref, keys), (value_ref, values)):
            total = sum(part.astype(F32) for part in found[1:]) + found[0]
            ref[:, first * HD : (first + count) * HD] = total.astype(BF16)


def per_device(queries, key_states, value_states, upstream, selected):
    slots = lax.axis_size("ctx")
    pipe, split = lax.axis_size("pipe"), lax.axis_size("head")
    tok_dev, rows_in = queries.shape[1], upstream.shape[1]
    heads = key_states.shape[2] // HD
    wide, rows = heads * HD, GROUP * tok_dev
    paired = heads == 4 and slots == 4
    groups = [(0, 2), (2, 2)] if paired else [(0, heads)]
    sends = [(0, 24), (24, 8)] if paired else [(0, heads * GROUP)]

    def swapped(value, mask):
        return lax.ppermute(value, "ctx", [(place, place ^ mask) for place in range(slots)])

    def across(part, step):
        route = [
            (sec * split + at, (sec - 1) % pipe * split + (at + step) % split)
            for sec in range(pipe)
            for at in range(split)
        ]
        return lax.ppermute(part, ("pipe", "head"), route)

    up, own_queries, own_keys, own_values = (
        in_hbm(value[0]) for value in (upstream, queries, key_states, value_states)
    )

    def cut_shapes(sends):
        return [shape((rows_in, count * HD)) for _, count in sends for _ in range(split)]

    *cut, own_kv = call(
        functools.partial(first_load_kernel, sends[:1], split, heads),
        "first_load",
        [*cut_shapes(sends[:1]), shape((tok_dev, 2 * wide))],
        [spec(HBM)] * 3,
        [spec()] * (split + 1),
        scratch_shapes=[pltpu.SemaphoreType.DMA((split + 2,))],
    )(up, own_keys, own_values)

    def gathered(own):
        found = {0: own}
        for mask in [1 << bit for bit in reversed(range(slots.bit_length() - 1))]:
            found.update({slot ^ mask: swapped(part, mask) for slot, part in found.items()})
        return [found[slot] for slot in range(1, slots)]

    def alone(own):
        return [own] * (slots - 1)

    others = slots - 1
    received = lax.cond(lax.axis_index("ctx") < slots, gathered, alone, own_kv)
    later = (len(sends) - 1) * split
    more = call(
        functools.partial(later_load_kernel, sends[1:], split, heads, others),
        "later_load",
        [*cut_shapes(sends[1:]), shape(queries.shape[1:])] + [shape((tok_dev, 2 * wide))] * others,
        [spec(HBM)] * (2 + others),
        [spec()] * (later + 1 + others),
        scratch_shapes=[pltpu.SemaphoreType.DMA((later + 1 + others,))],
    )(up, own_queries, *(in_hbm(part) for part in received))
    own_queries, kv = more[later], [own_kv, *more[later + 1 :]]
    cut = [*cut, *more[:later]]
    pieces = [
        [across(cut[at * split + step], step) for step in range(split)] for at in range(len(sends))
    ]

    def pieces_of(first, count):
        return [piece for at in overlaps(sends, first, count) for piece in pieces[at]]

    ins = (own_queries, selected[0], *kv)
    weights, outs = call(
        functools.partial(weights_kernel, slots, heads),
        "weights",
        [shape((heads, slots * tok_dev, rows)), shape((tok_dev, heads * HEAD_COLS), F32)],
        [spec()] * len(ins),
        [spec()] * 2,
    )(*ins)

    def sums_of(name, group, span, layout, grads=None, done=(), after=()):
        first, count = group
        used = pieces_of(first, count) if grads is None else grads
        before = done[0].shape[1] // (len(layout[0][2]) * HD) if done else 0
        ins = (weights, outs, own_queries, *kv[span[0] : span[1]], *done, *used, *after)
        results = [shape((tok_dev, count * HEAD_COLS))] if grads is None else []
        results.append(shape((count, (span[1] - span[0]) * tok_dev, rows)))
        results.extend(
            shape(((to - at) * tok_dev, len(kinds) * (before + count) * HD), dtype)
            for at, to, kinds, dtype in layout
        )
        return call(
            functools.partial(
                sums_kernel,
                span,
                first,
                count,
                sends,
                0 if grads is not None else split,
                before,
                [part[:3] for part in layout],
            ),
            name,
            results,
            [spec()] * len(ins),
            [spec()] * len(results),
        )(*ins)

    def query_of(score_grads, places):
        ins = (*score_grads, *kv)
        return call(
            functools.partial(query_kernel, slots, places, len(score_grads)),
            "query",
            shape((tok_dev, heads * HEAD_COLS)),
            [spec()] * len(ins),
            spec(HBM),
            scratch_shapes=[
                pltpu.VMEM((tok_dev, heads * HEAD_COLS), BF16),
                pltpu.SemaphoreType.DMA((heads,)),
            ],
        )(*ins)

    def added(keep, received, outs, *after):
        ins = (keep, received, *after)
        return call(
            functools.partial(add_kernel, len(outs)), "add", outs, [spec()] * len(ins), [spec()] * len(outs)
        )(*ins)

    both = ("key", "value")
    if paired:
        _, scores_a, keep_a, send = sums_of(
            "sums_early", (0, 2), (0, 4), [(0, 2, both, F32), (2, 4, both, BF16)]
        )
        arrived = swapped(send, 2)

        near = [(0, 1, both, F32), (1, 2, ("key",), BF16), (1, 2, ("value",), BF16)]
        kept, sent = (2, 3, both, F32), (3, 4, both, BF16)
        _, scores_b, *near_done, keep, send = sums_of("sums_middle", (2, 1), (0, 4), [*near, kept, sent])
        grads_c, scores_3, send = sums_of("sums_3", (3, 1), (3, 4), [sent], done=[send])
        scores_2, keep = sums_of("sums_2", (3, 1), (2, 3), [kept], [grads_c], [keep])
        part = (tok_dev, 4 * HD)
        (send,) = added(keep, swapped(send, 1), [shape(part)])
        scores_01, own, *sends_1 = sums_of("sums_01", (3, 1), (0, 2), near, [grads_c], near_done, [send])
        query_grad = query_of(
            [scores_a, scores_b, scores_01, scores_2, scores_3],
            [((0, 0),), ((0, 1),), ((1, 0),), ((2, 0), (3, 0), (4, 0))],
        )
        own_a, send_a = added(keep_a, arrived, [shape(part, F32), shape(part)], own)
        found = [own_a, swapped(send_a, 1)]
        found.extend([own, swapped(send, 2), *(swapped(part, 1) for part in sends_1)])
        counts = [(2, 0), (2, 1)]
    else:
        layout = [(0, 1, both, F32)] + [(slot, slot + 1, both, BF16) for slot in range(1, slots)]
        _, scores, own, *send = sums_of("sums", groups[0], (0, slots), layout)
        query_grad = query_of([scores], [((0, head),) for head in range(heads)])
        found = [own, *(swapped(part, slot) for slot, part in enumerate(send, 1))]
        counts = [(slots, 0)]

    key_grad, value_grad = call(
        functools.partial(finish_kernel, groups, counts),
        "finish",
        [shape((tok_dev, wide))] * 2,
        [spec()] * len(found),
        [spec()] * 2,
    )(*found)
    return query_grad[None], key_grad[None], value_grad[None]


def solution(mesh):
    split = P("pipe", "ctx", "head")
    placed = (split, split, split, P("pipe", ("ctx", "head"), None), P("pipe", "head", "ctx", None))
    return jax.shard_map(
        per_device, mesh=mesh, in_specs=placed, out_specs=(split, split, split), check_vma=False
    )
```
